256 devices in a mesh: ctx: 64 (over x, z_lo, y, core), head: 4 (over z_hi).
Axes of the slice: x: 4, y: 4, z: 8 (z_hi: 4, z_lo: 2; z = z_hi * 2 + z_lo), core: 2. Of those that a mesh axis runs over, the one named last changes fastest.
Arguments:
- layer_input: bfloat16 [8192, 8192], P('ctx'), may hold values from -6 to 6
- key_weight: bfloat16 [8192, 512], P(None, 'head'), may hold values from -0.0625 to 0.0625
- value_weight: bfloat16 [8192, 512], P(None, 'head'), may hold values from -0.0625 to 0.0625
- queries: bfloat16 [8192, 4096], P('ctx', 'head'), may hold values from -160 to 160
- out_grad: bfloat16 [8192, 4096], P('ctx', 'head'), may hold values from -192 to 192
- doc_start: int32 [8192], P('ctx'), may hold values from 0 to 8191, as said below
- block_order: int32 [128], replicated, may hold values from 0 to 127, as said below
Outputs:
- input_grad: bfloat16 [8192, 8192], P('ctx', 'head')
- query_grad: bfloat16 [8192, 4096], P('ctx', 'head')
The draws below stay inside these ranges and needn't reach their ends.
Inputs may be any that keep to these rules, and one draw needn't show every extreme that they name: `block_order`: entries 2d and 2d + 1 are j and 127 - j for some j < 64; all entries together are a permutation. doc_start of a row is the first position of the row's document, at most the row's own position; documents are runs of positions, at most 8 of them, and the last position forms a document of its own.
All inputs are finite; a program needn't handle non-finite values.
Results may differ from the reference program's by a relative error of at most 0.018.
Values may be sent and summed in bfloat16 or wider, within the bound.
No kernel may reach another device: no remote copies, remote signals or barrier semaphores. Data moves between devices by JAX's collectives and lax.ppermute only.
A program may use at most 128 MiB of HBM per device.

```python
import math
import jax
import jax.numpy as jnp
from jax import lax

D = 8192
HD = 128
GROUP = 8
TOK_DEV = 128
KV_HEADS = 4
Q_HEADS = 32
TOKENS = 8192
N_CTX = 64


def block_layout(key):
    shuffled = jax.random.permutation(jax.random.fold_in(key, 17), N_CTX).astype(jnp.int32)
    mirrored = 2 * N_CTX - 1 - shuffled
    return jnp.stack([shuffled, mirrored], axis=1).reshape(-1).astype(jnp.int32)


def draw_block_order(key, part):
    layout = block_layout(key)
    return layout


def draw_doc_start(key, part):
    layout = block_layout(key)
    key = jax.random.fold_in(key, 5)
    cut_points = jax.random.randint(key, (6,), 1, TOKENS, dtype=jnp.int32)
    places = jnp.arange(TOKENS, dtype=jnp.int32)
    begins = jnp.any(places[:, None] == cut_points[None, :], axis=1) | (places == 0) | (places == TOKENS - 1)
    first_pos = lax.cummax(jnp.where(begins, places, 0), axis=0)
    by_block = first_pos.reshape(2 * N_CTX, TOK_DEV // 2)
    return jnp.take(by_block, layout, axis=0).reshape(-1).astype(jnp.int32)


def draw_queries(key, part):
    key = jax.random.fold_in(key, 7)
    entry_key = jax.random.fold_in(key, 0)
    return jnp.clip(jax.random.normal(entry_key, (TOKENS, Q_HEADS * HD), jnp.float32), -6.0, 6.0).astype(jnp.bfloat16)


def block_scale(key, shape, shards, least, top_value):
    def one(axis_at, parts):
        heights = jax.random.uniform(jax.random.fold_in(jax.random.fold_in(key, 6), axis_at), (parts,), jnp.float32, least / len(shards), top_value / len(shards))
        return jnp.repeat(jnp.exp(heights), shape[axis_at] // parts).reshape((-1,) + (1,) * (len(shape) - axis_at - 1))

    level = one(*shards[0])
    for cut in shards[1:]:
        level = level * one(*cut)
    return level


def normal_values(own_key, extent, scale, limit, cuts=(), kind=jnp.bfloat16):
    factor_of = block_scale(own_key, extent, cuts, -0.22, 0.18) if cuts else 1.0
    values = jax.random.normal(own_key, extent, jnp.float32) * scale * factor_of
    return jnp.minimum(jnp.maximum(values, -limit), limit).astype(kind)


def setup_inputs(seed: int = 0) -> dict:
    splits = jax.random.split(jax.random.key(seed), 8)
    layer_input = normal_values(splits[0], (TOKENS, D), 1.0, 6.0, ((0, 64),))
    key_weight = normal_values(splits[1], (D, KV_HEADS * HD), D ** -0.5, 0.0625, ((1, 4),))
    value_weight = normal_values(splits[2], (D, KV_HEADS * HD), D ** -0.5, 0.0625, ((1, 4),))
    queries = draw_queries(jax.random.fold_in(splits[7], 71), 0)
    out_grad = normal_values(splits[4], (TOKENS, Q_HEADS * HD), 32.0, 192.0, ((0, 64), (1, 4)))
    doc_start = draw_doc_start(jax.random.fold_in(splits[7], 71), 0)
    block_order = draw_block_order(jax.random.fold_in(splits[7], 71), 0)
    return dict(layer_input=layer_input, key_weight=key_weight, value_weight=value_weight, queries=queries, out_grad=out_grad, doc_start=doc_start, block_order=block_order)


rope_base = 500000.0

def rotation_tables(positions, width):
    half_width = width // 2
    exponent = jnp.arange(half_width, dtype=jnp.float32) * (2.0 / width)
    frequency = jnp.exp(-math.log(rope_base) * exponent)
    angles = positions.astype(jnp.float32)[:, None] * frequency[None, :]
    return (jnp.cos(angles), jnp.sin(angles))

def rotate(vectors, cos_table, sin_table):
    half_width = vectors.shape[1] // 2
    first_half = vectors[:, :half_width]
    second_half = vectors[:, half_width:]
    return jnp.concatenate([first_half * cos_table - second_half * sin_table, second_half * cos_table + first_half * sin_table], axis=1)

def unrotate(vectors, cos_table, sin_table):
    half_width = vectors.shape[1] // 2
    first_half = vectors[:, :half_width]
    second_half = vectors[:, half_width:]
    return jnp.concatenate([first_half * cos_table + second_half * sin_table, second_half * cos_table - first_half * sin_table], axis=1)

def rounded(values):
    return lax.optimization_barrier(values.astype(jnp.bfloat16)).astype(jnp.float32)

def reference(layer_input, key_weight, value_weight, queries, out_grad, doc_start, block_order):
    block_len = TOK_DEV // 2
    scaling = 1.0 / math.sqrt(HD)
    highest = lax.Precision.HIGHEST
    offsets = jnp.arange(block_len, dtype=jnp.int32)
    positions = (block_order[:, None] * block_len + offsets[None, :]).reshape(-1).astype(jnp.int32)
    cos_table, sin_table = rotation_tables(positions, HD)
    pos_blocks = positions.reshape(N_CTX, TOK_DEV)
    start_blocks = doc_start.reshape(N_CTX, TOK_DEV)
    input_total = jnp.zeros((TOKENS, D), jnp.float32)
    query_parts = []
    for kv_head in range(KV_HEADS):
        key_cols = key_weight[:, kv_head * HD:(kv_head + 1) * HD]
        value_cols = value_weight[:, kv_head * HD:(kv_head + 1) * HD]
        key_raw = jnp.dot(layer_input, key_cols, preferred_element_type=jnp.float32)
        keys_f32 = rotate(key_raw, cos_table, sin_table)
        values_f32 = rounded(jnp.dot(layer_input, value_cols, preferred_element_type=jnp.float32))
        query_cols = queries[:, kv_head * GROUP * HD:(kv_head + 1) * GROUP * HD].reshape(N_CTX, TOK_DEV, GROUP, HD)
        grad_cols = out_grad[:, kv_head * GROUP * HD:(kv_head + 1) * GROUP * HD].reshape(N_CTX, TOK_DEV, GROUP, HD)

        def query_block(state_in, item_in):
            key_acc, value_acc = state_in
            query_tile, grad_tile, query_pos, query_first = item_in
            query_f32 = query_tile.astype(jnp.float32)
            grad_f32 = grad_tile.astype(jnp.float32)
            live_now = (positions[None, :] <= query_pos[:, None]) & (positions[None, :] >= query_first[:, None])
            live_three = live_now[:, None, :]
            scored = jnp.einsum('tgd,kd->tgk', query_f32, keys_f32, precision=highest) * scaling
            row_top = lax.optimization_barrier(jnp.max(jnp.where(live_three, scored, -jnp.inf), axis=-1))
            row_total = lax.optimization_barrier(jnp.sum(jnp.where(live_three, jnp.exp(scored - row_top[..., None]), 0.0), axis=-1))
            log_total = row_top + jnp.log(row_total)
            prob_tile = jnp.where(live_three, jnp.exp(scored - log_total[..., None]), 0.0)
            prob_grad = jnp.einsum('tgd,kd->tgk', grad_f32, values_f32)
            row_delta = lax.optimization_barrier(jnp.sum(prob_tile * prob_grad, axis=-1))
            score_grad = rounded(prob_tile * (prob_grad - row_delta[..., None]) * scaling)
            probs_half = rounded(prob_tile)
            query_grad = jnp.einsum('tgk,kd->tgd', score_grad, keys_f32, precision=highest)
            key_acc = key_acc + jnp.einsum('tgk,tgd->kd', score_grad, query_f32)
            value_acc = value_acc + jnp.einsum('tgk,tgd->kd', probs_half, grad_f32)
            return ((key_acc, value_acc), query_grad.astype(jnp.bfloat16))
        zeros_init = (jnp.zeros((TOKENS, HD), jnp.float32), jnp.zeros((TOKENS, HD), jnp.float32))
        (key_grad, value_grad), query_grad = lax.scan(query_block, zeros_init, (query_cols, grad_cols, pos_blocks, start_blocks))
        query_parts.append(query_grad.reshape(TOKENS, GROUP * HD))
        key_back = unrotate(key_grad, cos_table, sin_table).astype(jnp.bfloat16)
        value_back = value_grad.astype(jnp.bfloat16)
        input_total = input_total + jnp.dot(key_back, key_cols.T, preferred_element_type=jnp.float32)
        input_total = input_total + jnp.dot(value_back, value_cols.T, preferred_element_type=jnp.float32)
    return (input_total.astype(jnp.bfloat16), jnp.concatenate(query_parts, axis=1))
```

```python
import functools
import math

import jax
import jax.numpy as jnp
from jax import lax
from jax.experimental import pallas as pl
from jax.experimental.pallas import tpu as pltpu
from jax.sharding import PartitionSpec as P

rope_base = 500000.0
big_negative = -1e30
n_ctx = 64
n_head = 4
block_len = 64
key_span = 256
log2e = 1.4426950408889634


def split_index(c):
    return c // 16, (c // 8) % 2, (c // 2) % 4, c % 2


def join_index(x, z, y, core):
    return ((x * 2 + z) * 4 + y) * 2 + core


def make_perm(target):
    return [(c, join_index(*target(*split_index(c)))) for c in range(n_ctx)]


core_perm = make_perm(lambda x, z, y, k: (x, z, y, 1 - k))
z_perm = make_perm(lambda x, z, y, k: (x, 1 - z, y, k))


def first_perm(s):
    return make_perm(
        lambda x, z, y, k: ((x + s) % 4, z, y, k) if k == 0 else (x, z, (y + s) % 4, k)
    )


def second_perm(s):
    return make_perm(
        lambda x, z, y, k: (x, z, (y + s) % 4, k) if k == 0 else ((x + s) % 4, z, y, k)
    )


def head_perm(s):
    return [(h, (h + s) % n_head) for h in range(n_head)]


def rotation_tables(positions, width):
    half_width = width // 2
    exponent = jnp.arange(half_width, dtype=jnp.float32) * (2.0 / width)
    frequency = jnp.exp(-math.log(rope_base) * exponent)
    angles = positions.astype(jnp.float32)[:, None] * frequency[None, :]
    return (jnp.cos(angles), jnp.sin(angles))


def rotate(vectors, cos_table, sin_table):
    half_width = vectors.shape[1] // 2
    a = vectors[:, :half_width]
    b = vectors[:, half_width:]
    return jnp.concatenate([a * cos_table - b * sin_table, b * cos_table + a * sin_table], axis=1)


def unrotate(vectors, cos_table, sin_table):
    return rotate(vectors, cos_table, -sin_table)


def attention_kernel(
    place_ref,
    order_ref,
    *refs,
    scaling,
    tokens,
):
    pieces = refs[:8]
    qt_ref, dot_ref, q_ref, do_ref, pos_ref, start_ref = refs[8:14]
    outs = refs[14:22]
    dqt_ref = refs[22]
    kv, acc, dq_acc, sem = refs[23:]
    x, z, y, core = place_ref[0], place_ref[1], place_ref[2], place_ref[3]

    def sequence_block(piece, i):
        s2 = piece % 4
        holder = core if piece < 4 else 1 - core
        s1 = i // 4
        src_z = jnp.where((i // 2) % 2 == 0, z, 1 - z)
        src_core = jnp.where(i % 2 == 0, holder, 1 - holder)
        dx = jnp.where(holder == 0, s1, s2)
        dy = jnp.where(holder == 0, s2, s1)
        src_x = (x + 4 - dx) % 4
        src_y = (y + 4 - dy) % 4
        stored = (((src_x * 2 + src_z) * 4 + src_y) * 2 + src_core) * 2 + holder
        return order_ref[stored]

    for piece in range(8):

        def fetch(i, carry, piece=piece):
            seq = sequence_block(piece, i)
            pltpu.make_async_copy(
                pieces[piece].at[pl.ds(pl.multiple_of(i * block_len, block_len), block_len), :],
                kv.at[pl.ds(pl.multiple_of(seq * block_len, block_len), block_len), :],
                sem,
            ).start()
            return carry

        lax.fori_loop(0, 16, fetch, 0)

    acc[...] = jnp.zeros_like(acc)
    pltpu.make_async_copy(kv, kv, sem).wait()

    half = q_ref.shape[0] // 2
    head_dim = q_ref.shape[1]
    factor = scaling * log2e
    for part in range(2):
        cols = pl.ds(part * half, half)
        own_block = place_ref[4 + part]
        first = place_ref[6 + part] // key_span
        last = own_block * block_len // key_span + 1
        pos = pos_ref[:, cols]
        start = start_ref[:, cols]

        def tile(kt):
            rows = pl.ds(pl.multiple_of(kt * key_span, key_span), key_span)
            key = kv[rows, : 2 * head_dim]
            value = kv[rows, 2 * head_dim :]
            score = (
                jnp.dot(key, qt_ref[:, cols], preferred_element_type=jnp.float32) * factor
            )
            prob_grad = jnp.dot(value, dot_ref[:, cols], preferred_element_type=jnp.float32)
            key_pos = kt * key_span + lax.broadcasted_iota(jnp.int32, (key_span, half), 0)
            live = (key_pos <= pos) & (key_pos >= start)
            return rows, key, score, prob_grad, live

        def stats(kt, carried):
            top, total, weighted = carried
            _, _, score, prob_grad, live = tile(kt)
            score = jnp.where(live, score, big_negative)
            new_top = jnp.maximum(top, jnp.max(score, axis=0, keepdims=True))
            growth = jnp.exp2(score - new_top)
            faded = jnp.exp2(top - new_top)
            return (
                new_top,
                total * faded + jnp.sum(growth, axis=0, keepdims=True),
                weighted * faded + jnp.sum(growth * prob_grad, axis=0, keepdims=True),
            )

        row = (1, half)
        top, total, weighted = lax.fori_loop(
            first,
            last,
            stats,
            (
                jnp.full(row, big_negative, jnp.float32),
                jnp.zeros(row, jnp.float32),
                jnp.zeros(row, jnp.float32),
            ),
        )
        log_total = top + jnp.log2(total)
        delta = weighted / total
        dq_acc[...] = jnp.zeros_like(dq_acc)

        def grads(kt, carry):
            rows, key, score, prob_grad, live = tile(kt)
            prob = jnp.where(live, jnp.exp2(score - log_total), 0.0)
            score_grad = (prob * (prob_grad - delta) * scaling).astype(jnp.bfloat16)
            acc[rows, :head_dim] += jnp.dot(
                score_grad, q_ref[cols, :], preferred_element_type=jnp.float32
            )
            acc[rows, head_dim:] += jnp.dot(
                prob.astype(jnp.bfloat16), do_ref[cols, :], preferred_element_type=jnp.float32
            )
            dq_acc[...] += jnp.dot(key.T, score_grad, preferred_element_type=jnp.float32)
            return carry

        lax.fori_loop(first, last, grads, 0)
        dqt_ref[:, cols] = dq_acc[:head_dim, :] + dq_acc[head_dim:, :]

    for piece in range(8):

        def store(i, carry, piece=piece):
            seq = sequence_block(piece, i)
            outs[piece][pl.ds(pl.multiple_of(i * block_len, block_len), block_len), :] = acc[
                pl.ds(pl.multiple_of(seq * block_len, block_len), block_len), :
            ].astype(jnp.bfloat16)
            return carry

        lax.fori_loop(0, 16, store, 0)


def attention(place, order, pieces, qt, dot_, q, do, pos, start, scaling, tokens):
    head_dim = q.shape[1]
    rows = q.shape[0]
    smem = pl.BlockSpec(memory_space=pltpu.SMEM)
    vmem = pl.BlockSpec(memory_space=pltpu.VMEM)
    piece_rows = tokens // 8
    return pl.pallas_call(
        functools.partial(attention_kernel, scaling=scaling, tokens=tokens),
        out_shape=[jax.ShapeDtypeStruct((piece_rows, 2 * head_dim), jnp.bfloat16)] * 8
        + [jax.ShapeDtypeStruct((head_dim, rows), jnp.float32)],
        in_specs=[smem, smem] + [pl.BlockSpec(memory_space=pl.ANY)] * 8 + [vmem] * 6,
        out_specs=[vmem] * 9,
        scratch_shapes=[
            pltpu.VMEM((tokens, 3 * head_dim), jnp.bfloat16),
            pltpu.VMEM((tokens, 2 * head_dim), jnp.float32),
            pltpu.VMEM((2 * head_dim, rows // 2), jnp.float32),
            pltpu.SemaphoreType.DMA,
        ],
        compiler_params=pltpu.CompilerParams(vmem_limit_bytes=48 * 1024 * 1024),
        cost_estimate=pl.CostEstimate(
            flops=10 * rows * tokens * head_dim,
            bytes_accessed=12 * 1024 * 1024,
            transcendentals=rows * tokens,
        ),
    )(place, order, *pieces, qt, dot_, q, do, pos, start)


def shards(layer_input, key_weight, value_weight, queries, out_grad, doc_start, block_order):
    f32, bf16 = jnp.float32, jnp.bfloat16
    row_count = layer_input.shape[0]
    tokens = row_count * n_ctx
    head_dim = key_weight.shape[1]
    width = key_weight.shape[0]
    groups = queries.shape[1] // head_dim
    scaling = 1.0 / math.sqrt(head_dim)
    device = lax.axis_index("ctx")
    head = lax.axis_index("head")
    x, z, y, core = split_index(device)
    own_blocks = lax.dynamic_slice_in_dim(block_order, 2 * device, 2)
    own_pos = (
        own_blocks[:, None] * block_len + jnp.arange(block_len, dtype=jnp.int32)[None, :]
    ).reshape(-1)
    cos_own, sin_own = rotation_tables(own_pos, head_dim)

    def send(v, perm):
        return lax.ppermute(v, "ctx", perm)

    key_raw = jnp.dot(layer_input, key_weight, preferred_element_type=f32)
    keys = rotate(key_raw, cos_own, sin_own)
    key_hi = lax.reduce_precision(keys, 8, 7)
    key_lo = keys - key_hi
    values = jnp.dot(layer_input, value_weight, preferred_element_type=f32)
    local = jnp.concatenate(
        [key_hi.astype(bf16), key_lo.astype(bf16), values.astype(bf16)], axis=1
    ).reshape(2, block_len, 3 * head_dim)

    kept = lax.dynamic_index_in_dim(local, core, 0, keepdims=False)
    given = lax.dynamic_index_in_dim(local, 1 - core, 0, keepdims=False)
    pair = jnp.concatenate([kept, send(given, core_perm)], axis=0)
    node = jnp.concatenate([pair, send(pair, z_perm)], axis=0)
    line = jnp.concatenate([node] + [send(node, first_perm(s)) for s in (1, 2, 3)], axis=0)
    mine = [line] + [send(line, second_perm(s)) for s in (1, 2, 3)]
    others = [send(v, core_perm) for v in mine]

    out_width = width // n_head
    half_width = out_width // 2
    both_weights = jnp.concatenate([key_weight, value_weight], axis=1).reshape(
        n_head, 2, half_width, 2 * head_dim
    )

    def weight_part(to_head, part):
        return lax.dynamic_slice(
            both_weights, (to_head, part, 0, 0), (1, 1, half_width, 2 * head_dim)
        )[0, 0]

    core_is_zero = core == 0
    weights = [lax.dynamic_index_in_dim(both_weights, head, 0, keepdims=False)]
    for s in (1, 2, 3):
        half_own = lax.ppermute(weight_part((head + s) % n_head, core), "head", head_perm(s))
        half_other = send(half_own, core_perm)
        weights.append(
            jnp.where(
                core_is_zero,
                jnp.stack([half_own, half_other]),
                jnp.stack([half_other, half_own]),
            )
        )

    def by_block(v):
        return v.reshape(2, block_len, groups, head_dim)

    q_blocks = by_block(queries)
    g_blocks = by_block(out_grad)
    rows = row_count * groups
    q_rows = q_blocks.transpose(0, 2, 1, 3).reshape(rows, head_dim)
    g_rows = g_blocks.transpose(0, 2, 1, 3).reshape(rows, head_dim)
    q_cols = q_blocks.transpose(3, 0, 2, 1).reshape(head_dim, rows)
    g_cols = g_blocks.transpose(3, 0, 2, 1).reshape(head_dim, rows)
    q_cols = jnp.concatenate([q_cols, q_cols], axis=0)

    def per_column(v):
        return jnp.broadcast_to(v.reshape(2, 1, block_len), (2, groups, block_len)).reshape(1, rows)

    starts = doc_start.reshape(2, block_len)[:, 0]
    place = jnp.concatenate([jnp.stack([x, z, y, core]), own_blocks, starts]).astype(jnp.int32)
    result = attention(
        place,
        block_order,
        mine + others,
        q_cols,
        g_cols,
        q_rows,
        g_rows,
        per_column(own_pos),
        per_column(doc_start),
        scaling,
        tokens,
    )
    parts, dq_cols = result[:8], result[8]
    query_grad = (
        dq_cols.reshape(head_dim, 2, groups, block_len)
        .transpose(1, 3, 2, 0)
        .reshape(row_count, groups * head_dim)
        .astype(bf16)
    )

    def added(*terms):
        total = terms[0].astype(f32)
        for term in terms[1:]:
            total = total + term.astype(f32)
        return total

    merged = [added(parts[s], send(parts[4 + s], core_perm)).astype(bf16) for s in range(4)]
    line_grad = added(merged[0], *[send(merged[s], second_perm(4 - s)) for s in (1, 2, 3)])
    line_grad = line_grad.astype(bf16).reshape(4, 4 * block_len, 2 * head_dim)
    node_grad = added(line_grad[0], *[send(line_grad[s], first_perm(4 - s)) for s in (1, 2, 3)])
    node_grad = node_grad.astype(bf16).reshape(2, 2 * block_len, 2 * head_dim)
    pair_grad = added(node_grad[0], send(node_grad[1], z_perm)).reshape(
        2, block_len, 2 * head_dim
    )
    other_grad = send(pair_grad[1].astype(bf16), core_perm).astype(f32)
    summed = jnp.where(
        core_is_zero,
        jnp.concatenate([pair_grad[0], other_grad]),
        jnp.concatenate([other_grad, pair_grad[0]]),
    )
    key_back = unrotate(summed[:, :head_dim], cos_own, sin_own).astype(bf16)
    back = jnp.concatenate([key_back, summed[:, head_dim:].astype(bf16)], axis=1)
    backs = [back] + [lax.ppermute(back, "head", head_perm(s)) for s in (1, 2, 3)]
    contract = (((1,), (1,)), ((), ()))
    total = jnp.zeros((row_count, out_width), f32)
    for b, w in zip(backs, weights):
        total = total + lax.dot_general(
            b, w.reshape(out_width, 2 * head_dim), contract, preferred_element_type=f32
        )
    return (total.astype(bf16), query_grad)


def solution(mesh):
    return jax.shard_map(
        shards,
        mesh=mesh,
        in_specs=(
            P("ctx", None),
            P(None, "head"),
            P(None, "head"),
            P("ctx", "head"),
            P("ctx", "head"),
            P("ctx"),
            P(),
        ),
        out_specs=(P("ctx", "head"), P("ctx", "head")),
        check_vma=False,
    )
```

```python
import functools
import math

import jax
import jax.numpy as jnp
from jax import lax
from jax.experimental import pallas as pl
from jax.experimental.pallas import tpu as pltpu
from jax.sharding import Mesh
from jax.sharding import PartitionSpec as P

rope_base = 500000.0
big_negative = -1e30
n_ctx = 64
n_head = 4
block_len = 64
key_span = 256
granule = 16
log2e = 1.4426950408889634


swap = [(0, 1), (1, 0)]
both_swap = [(0, 3), (1, 2), (2, 1), (3, 0)]


def head_perm(s):
    return [(h, (h + s) % n_head) for h in range(n_head)]


def rotation_tables(positions, width):
    half_width = width // 2
    exponent = jnp.arange(half_width, dtype=jnp.float32) * (2.0 / width)
    frequency = jnp.exp(-math.log(rope_base) * exponent)
    angles = positions.astype(jnp.float32)[:, None] * frequency[None, :]
    return (jnp.cos(angles), jnp.sin(angles))


def rotate(vectors, cos_table, sin_table):
    half_width = vectors.shape[1] // 2
    a = vectors[:, :half_width]
    b = vectors[:, half_width:]
    return jnp.concatenate([a * cos_table - b * sin_table, b * cos_table + a * sin_table], axis=1)


def unrotate(vectors, cos_table, sin_table):
    return rotate(vectors, cos_table, -sin_table)


def granule_rows(index):
    return pl.ds(pl.multiple_of(index * granule, granule), granule)


def load_operands(order_ref, gathered, packs, kv, q_rows, g_rows, starts):
    tokens = kv.shape[0] - key_span
    kv[tokens:, :] = jnp.zeros_like(kv[tokens:, :])

    def fetch(i, carry):
        kv[granule_rows(order_ref[i]), :] = gathered[granule_rows(i), :]
        return carry

    lax.fori_loop(0, tokens // granule, fetch, 0, unroll=8)
    head_dim = q_rows.shape[1]
    half = starts.shape[1]
    for rel in range(4):
        pack = packs[rel]
        code = pack[256:272, :].astype(jnp.float32)
        start = (code[0:1, :] * 128.0 + code[1:2, :]).astype(jnp.int32)
        for block in range(2):
            part = rel * 2 + block
            starts[part : part + 1, :] = start[:, block * half : (block + 1) * half]
            for group in range(half // block_len):
                to = pl.ds(part * half + group * block_len, block_len)
                cols = pl.ds(group * head_dim, head_dim)
                q_rows[to, :] = pack[block * block_len : (block + 1) * block_len, cols]
                g_rows[to, :] = pack[128 + block * block_len : 128 + (block + 1) * block_len, cols]


def query_part(place_ref, part, half):
    block = place_ref[1 + part]
    first_block = place_ref[9 + part] // block_len
    tiles = ((block - first_block + 1) * granule + key_span - 1) // key_span
    lane = lax.broadcasted_iota(jnp.int32, (1, half), 1)
    return first_block, tiles, place_ref[17 + part], block * block_len + lane % block_len


chunk = 512
contract_last = (((1,), (1,)), ((), ()))


def tile_rows(kt, first_block, place_ref):
    base = first_block * granule + kt * key_span
    offset = (first_block + kt * (key_span // granule)) * block_len + place_ref[0] * granule
    return pl.ds(pl.multiple_of(base, granule), key_span), offset


def fill_positions(key_rel):
    row = lax.broadcasted_iota(jnp.int32, key_rel.shape, 0)
    key_rel[...] = (row // granule) * block_len + row % granule


def chunk_terms(key, value, q_wide, g_part, pos, start, key_rel, factor):
    score = lax.dot_general(key, q_wide, contract_last, preferred_element_type=jnp.float32) * factor
    prob_grad = lax.dot_general(value, g_part, contract_last, preferred_element_type=jnp.float32)
    live = (key_rel <= pos) & (key_rel >= start)
    return score, prob_grad, live


def stats_kernel(place_ref, order_ref, *refs, factor):
    gathered, packs, stats_ref = refs[0], refs[1:5], refs[5]
    kv, q_rows, g_rows, starts, key_rel = refs[6:]
    load_operands(order_ref, gathered, packs, kv, q_rows, g_rows, starts)
    half = starts.shape[1]
    head_dim = q_rows.shape[1]
    fill_positions(key_rel)

    def one_part(part, carry):
        first_block, tiles, slot, pos = query_part(place_ref, part, half)
        cols = pl.ds(pl.multiple_of(part * half, half), half)
        start = starts[pl.ds(part, 1), :]

        def stats(kt, carried):
            rows, offset = tile_rows(kt, first_block, place_ref)
            key = kv[rows, : 2 * head_dim]
            value = kv[rows, 2 * head_dim :]
            result = []
            for c in range(half // chunk):
                top, total, weighted = carried[c]
                at = slice(c * chunk, (c + 1) * chunk)
                to = pl.ds(pl.multiple_of(part * half + c * chunk, chunk), chunk)
                q_part = q_rows[to, :]
                score, prob_grad, live = chunk_terms(
                    key,
                    value,
                    jnp.concatenate([q_part, q_part], axis=1),
                    g_rows[to, :],
                    pos[:, at] - offset,
                    start[:, at] - offset,
                    key_rel[...],
                    factor,
                )
                score = jnp.where(live, score, big_negative)
                new_top = jnp.maximum(top, jnp.max(score, axis=0, keepdims=True))
                growth = jnp.exp2(score - new_top)
                faded = jnp.exp2(top - new_top)
                result.append(
                    (
                        new_top,
                        total * faded + jnp.sum(growth, axis=0, keepdims=True),
                        weighted * faded + jnp.sum(growth * prob_grad, axis=0, keepdims=True),
                    )
                )
            return tuple(result)

        row = (1, chunk)
        zero = jnp.zeros(row, jnp.float32)
        init = (jnp.full(row, big_negative, jnp.float32), zero, zero)
        carried = lax.fori_loop(0, tiles, stats, (init,) * (half // chunk))
        top, total, weighted = (jnp.concatenate(v, axis=1) for v in zip(*carried))
        stats_ref[pl.ds(slot, 1), :] = top + jnp.log2(total)
        stats_ref[pl.ds(8 + slot, 1), :] = weighted / total
        return carry

    lax.fori_loop(0, 8, one_part, 0)


def grads_kernel(place_ref, order_ref, *refs, factor, scaling):
    gathered, packs, stats = refs[0], refs[1:5], refs[5:9]
    out_ref, dq_ref = refs[9:11]
    kv, q_rows, g_rows, starts, key_rel, acc, dq_acc, logs, deltas = refs[11:]
    load_operands(order_ref, gathered, packs, kv, q_rows, g_rows, starts)
    half = starts.shape[1]
    head_dim = q_rows.shape[1]
    acc[...] = jnp.zeros_like(acc)
    fill_positions(key_rel)

    top = jnp.maximum(
        jnp.maximum(stats[0][:8, :], stats[1][:8, :]), jnp.maximum(stats[2][:8, :], stats[3][:8, :])
    )
    total = jnp.zeros_like(top)
    weighted = jnp.zeros_like(top)
    for s in stats:
        share = jnp.exp2(s[:8, :] - top)
        total = total + share
        weighted = weighted + share * s[8:, :]
    logs[...] = top + jnp.log2(total)
    deltas[...] = weighted / total

    def one_part(part, carry):
        first_block, tiles, slot, pos = query_part(place_ref, part, half)
        cols = pl.ds(pl.multiple_of(part * half, half), half)
        start = starts[pl.ds(part, 1), :]
        log_total = logs[pl.ds(slot, 1), :]
        delta = deltas[pl.ds(slot, 1), :]
        dq_acc[...] = jnp.zeros_like(dq_acc)

        def grads(kt, carry):
            rows, offset = tile_rows(kt, first_block, place_ref)
            key = kv[rows, : 2 * head_dim]
            value = kv[rows, 2 * head_dim :]
            key_t = key.T
            key_sum = acc[rows, :head_dim]
            value_sum = acc[rows, head_dim:]
            for c in range(half // chunk):
                at = slice(c * chunk, (c + 1) * chunk)
                to = pl.ds(pl.multiple_of(part * half + c * chunk, chunk), chunk)
                q_part = q_rows[to, :]
                g_part = g_rows[to, :]
                score, prob_grad, live = chunk_terms(
                    key,
                    value,
                    jnp.concatenate([q_part, q_part], axis=1),
                    g_part,
                    pos[:, at] - offset,
                    start[:, at] - offset,
                    key_rel[...],
                    factor,
                )
                prob = jnp.where(live, jnp.exp2(score - log_total[:, at]), 0.0)
                score_grad = (prob * ((prob_grad - delta[:, at]) * scaling)).astype(jnp.bfloat16)
                key_sum += jnp.dot(score_grad, q_part, preferred_element_type=jnp.float32)
                value_sum += jnp.dot(
                    prob.astype(jnp.bfloat16), g_part, preferred_element_type=jnp.float32
                )
                dq_acc[:, at] += jnp.dot(key_t, score_grad, preferred_element_type=jnp.float32)
            acc[rows, :head_dim] = key_sum
            acc[rows, head_dim:] = value_sum
            return carry

        lax.fori_loop(0, tiles, grads, 0)
        dq = (dq_acc[:head_dim, :] + dq_acc[head_dim:, :]).T
        to = pl.ds(pl.multiple_of(part * block_len, block_len), block_len)
        for group in range(half // block_len):
            dq_ref[to, group * head_dim : (group + 1) * head_dim] = dq[
                group * block_len : (group + 1) * block_len, :
            ]
        return carry

    lax.fori_loop(0, 8, one_part, 0)

    def store(i, carry):
        out_ref[granule_rows(i), :] = acc[granule_rows(order_ref[i]), :].astype(jnp.bfloat16)
        return carry

    lax.fori_loop(0, out_ref.shape[0] // granule, store, 0, unroll=8)


def kernel_scratch(quarter, head_dim, rows):
    half = rows // 2
    return [
        pltpu.VMEM((quarter + key_span, 3 * head_dim), jnp.bfloat16),
        pltpu.VMEM((4 * rows, head_dim), jnp.bfloat16),
        pltpu.VMEM((4 * rows, head_dim), jnp.bfloat16),
        pltpu.VMEM((8, half), jnp.int32),
        pltpu.VMEM((key_span, chunk), jnp.int32),
    ]


def run_stats(place, order, gathered, packs, scaling, tokens, head_dim, rows):
    smem = pl.BlockSpec(memory_space=pltpu.SMEM)
    vmem = pl.BlockSpec(memory_space=pltpu.VMEM)
    return pl.pallas_call(
        functools.partial(stats_kernel, factor=scaling * log2e),
        out_shape=jax.ShapeDtypeStruct((16, rows // 2), jnp.float32),
        in_specs=[smem, smem] + [vmem] * 5,
        out_specs=vmem,
        scratch_shapes=kernel_scratch(tokens // 4, head_dim, rows),
        compiler_params=pltpu.CompilerParams(vmem_limit_bytes=32 * 1024 * 1024),
        cost_estimate=pl.CostEstimate(
            flops=8 * rows * tokens * head_dim,
            bytes_accessed=4 * 1024 * 1024,
            transcendentals=rows * tokens // 2,
        ),
    )(place, order, gathered, *packs)


def run_grads(place, order, gathered, packs, stats, scaling, tokens, head_dim, rows):
    smem = pl.BlockSpec(memory_space=pltpu.SMEM)
    vmem = pl.BlockSpec(memory_space=pltpu.VMEM)
    quarter = tokens // 4
    half = rows // 2
    return pl.pallas_call(
        functools.partial(grads_kernel, factor=scaling * log2e, scaling=scaling),
        out_shape=[
            jax.ShapeDtypeStruct((quarter, 2 * head_dim), jnp.bfloat16),
            jax.ShapeDtypeStruct((8 * block_len, (half // block_len) * head_dim), jnp.float32),
        ],
        in_specs=[smem, smem] + [vmem] * 9,
        out_specs=[vmem] * 2,
        scratch_shapes=kernel_scratch(quarter, head_dim, rows)
        + [
            pltpu.VMEM((quarter + key_span, 2 * head_dim), jnp.float32),
            pltpu.VMEM((2 * head_dim, half), jnp.float32),
            pltpu.VMEM((8, half), jnp.float32),
            pltpu.VMEM((8, half), jnp.float32),
        ],
        compiler_params=pltpu.CompilerParams(vmem_limit_bytes=40 * 1024 * 1024),
        cost_estimate=pl.CostEstimate(
            flops=16 * rows * tokens * head_dim,
            bytes_accessed=8 * 1024 * 1024,
            transcendentals=rows * tokens // 2,
        ),
    )(place, order, gathered, *packs, *stats)


def product_kernel(place_ref, back_ref, key_ref, value_ref, *refs):
    near, far, near_core, far_core, out_ref = refs
    head = place_ref[0]
    contract = (((1,), (1,)), ((), ()))
    width = 2 * key_ref.shape[1]
    span = near.shape[1]

    def share(source):
        return back_ref[:, pl.ds(pl.multiple_of(source * width, width), width)]

    def times(left, right):
        return lax.dot_general(left, right, contract, preferred_element_type=jnp.float32)

    backs = [share((head + n_head - s) % n_head) for s in range(n_head)]
    for rel, piece in enumerate((near, near_core, far, far_core)):
        at = pl.ds(pl.multiple_of(place_ref[1 + rel] * span, span), span)
        own = jnp.concatenate([key_ref[at, :], value_ref[at, :]], axis=1)
        total = times(backs[0], own)
        for s in range(1, n_head):
            total += times(backs[s], piece[s - 1])
        out_ref[:, at] = total.astype(jnp.bfloat16)


def run_product(place, back, key_own, value_own, pieces):
    smem = pl.BlockSpec(memory_space=pltpu.SMEM)
    vmem = pl.BlockSpec(memory_space=pltpu.VMEM)
    out_width = key_own.shape[0]
    return pl.pallas_call(
        product_kernel,
        out_shape=jax.ShapeDtypeStruct((back.shape[0], out_width), jnp.bfloat16),
        in_specs=[smem] + [vmem] * 7,
        out_specs=vmem,
        compiler_params=pltpu.CompilerParams(vmem_limit_bytes=24 * 1024 * 1024),
        cost_estimate=pl.CostEstimate(
            flops=2 * back.shape[0] * back.shape[1] * out_width,
            bytes_accessed=5 * 1024 * 1024,
            transcendentals=0,
        ),
    )(place, back, key_own, value_own, *pieces)


def flip(v, axis, when):
    return jnp.where(when, jnp.flip(v, axis), v)


def shards(layer_input, key_weight, value_weight, queries, out_grad, doc_start, block_order):
    f32, bf16 = jnp.float32, jnp.bfloat16
    row_count = layer_input.shape[0]
    tokens = row_count * n_ctx
    head_dim = key_weight.shape[1]
    width = key_weight.shape[0]
    groups = queries.shape[1] // head_dim
    rows = row_count * groups
    scaling = 1.0 / math.sqrt(head_dim)
    x, y = lax.axis_index("x"), lax.axis_index("y")
    z, core, head = lax.axis_index("zl"), lax.axis_index("core"), lax.axis_index("head")
    z_is_one, core_is_one = z == 1, core == 1

    def pick(v, index, axis):
        return lax.dynamic_index_in_dim(v, index, axis, keepdims=False)

    order = block_order.reshape(4, 2, 4, 2, 2).transpose(0, 2, 1, 3, 4)
    order = flip(flip(order, 2, z_is_one), 3, core_is_one)
    node_blocks = pick(pick(order, x, 0), y, 0).reshape(8)

    own_blocks = node_blocks[:2]
    own_pos = (
        own_blocks[:, None] * block_len + jnp.arange(block_len, dtype=jnp.int32)[None, :]
    ).reshape(-1)
    cos_own, sin_own = rotation_tables(own_pos, head_dim)
    key_raw = jnp.dot(layer_input, key_weight, preferred_element_type=f32)
    keys = rotate(key_raw, cos_own, sin_own)
    key_hi = lax.reduce_precision(keys, 8, 7)
    key_lo = keys - key_hi
    values = jnp.dot(layer_input, value_weight, preferred_element_type=f32)
    local = jnp.concatenate(
        [key_hi.astype(bf16), key_lo.astype(bf16), values.astype(bf16)], axis=1
    ).reshape(2, 2, 2, granule, 3 * head_dim)

    pair = jnp.stack(
        [pick(local, core, 2), lax.ppermute(pick(local, 1 - core, 2), "core", swap)]
    )
    node = jnp.stack([pick(pair, z, 2), lax.ppermute(pick(pair, 1 - z, 2), "zl", swap)])
    node = node.reshape(1, row_count, 3 * head_dim)

    def per_column(v):
        return jnp.broadcast_to(v.reshape(2, 1, block_len), (2, groups, block_len)).reshape(1, rows)

    start_cols = per_column(doc_start)
    start_code = jnp.concatenate(
        [start_cols // 128, start_cols % 128, jnp.zeros((14, rows), jnp.int32)], axis=0
    ).astype(bf16)
    pack_own = jnp.concatenate([queries, out_grad, start_code], axis=0)
    node, pack_sent = lax.optimization_barrier((node, pack_own))
    pack_z = lax.ppermute(pack_sent, "zl", swap)
    packs = [
        pack_own,
        lax.ppermute(pack_own, "core", swap),
        pack_z,
        lax.ppermute(pack_z, "core", swap),
    ]

    out_width = width // n_head
    span = out_width // 4
    quarter = z * 2 + core

    def weight_part(to_head):
        at = to_head * out_width + quarter * span
        return jnp.concatenate(
            [lax.dynamic_slice_in_dim(w, at, span) for w in (key_weight, value_weight)], axis=1
        )

    weight_parts = [weight_part((head + s) % n_head) for s in (1, 2, 3)]
    key_own = lax.dynamic_slice_in_dim(key_weight, head * out_width, out_width)
    value_own = lax.dynamic_slice_in_dim(value_weight, head * out_width, out_width)
    node, weight_parts = lax.optimization_barrier((node, weight_parts))
    weights_near = [
        lax.ppermute(w, "head", head_perm(s)) for w, s in zip(weight_parts, (1, 2, 3))
    ]

    gathered = lax.all_to_all(
        jnp.broadcast_to(node, (16, row_count, 3 * head_dim)), ("x", "y"), 0, 0
    ).reshape(tokens // 4, 3 * head_dim)

    codes = jnp.stack([p[256:258, :: rows // 2] for p in packs]).astype(f32)
    firsts = (codes[:, 0] * 128.0 + codes[:, 1]).astype(jnp.int32).reshape(8)
    slots = jnp.arange(8, dtype=jnp.int32).reshape(2, 2, 2)
    slots = flip(flip(slots, 0, z_is_one), 1, core_is_one).reshape(8)
    place = jnp.concatenate([quarter[None], node_blocks, firsts, slots]).astype(jnp.int32)
    table = order.reshape(tokens // block_len)
    stats = run_stats(place, table, gathered, packs, scaling, tokens, head_dim, rows)
    stats_all = [
        stats,
        lax.ppermute(stats, "core", swap),
        lax.ppermute(stats, "zl", swap),
        lax.ppermute(stats, ("zl", "core"), both_swap),
    ]
    stats_all, weights_near = lax.optimization_barrier((stats_all, weights_near))
    weights_near = jnp.stack(weights_near)
    weights_far = lax.ppermute(weights_near, "zl", swap)
    grads, dq = run_grads(
        place, table, gathered, packs, stats_all, scaling, tokens, head_dim, rows
    )
    grads, weights_far = lax.optimization_barrier((grads, weights_far))
    weights = [
        weights_near,
        weights_far,
        lax.ppermute(weights_near, "core", swap),
        lax.ppermute(weights_far, "core", swap),
    ]

    grads = lax.all_to_all(
        grads.reshape(16, row_count, 2 * head_dim), ("x", "y"), 0, 0
    )
    grads = jnp.sum(grads.astype(f32), axis=0)
    quarter_pos = (
        node_blocks[:, None] * block_len
        + quarter * granule
        + jnp.arange(granule, dtype=jnp.int32)[None, :]
    ).reshape(-1)
    cos_node, sin_node = rotation_tables(quarter_pos, head_dim)
    key_back = unrotate(grads[:, :head_dim], cos_node, sin_node).astype(bf16)
    back = jnp.concatenate([key_back, grads[:, head_dim:].astype(bf16)], axis=1)

    back = back.reshape(2, 2, 2, granule, 2 * head_dim)
    back = jnp.stack([back[:, 0], lax.ppermute(back[:, 1], "core", swap)], axis=1)
    back = flip(flip(back, 0, z_is_one), 1, core_is_one)
    back = jnp.broadcast_to(back[:, None], (2, n_head) + back.shape[1:]).reshape(
        8, row_count // 2, 2 * head_dim
    )
    back = lax.all_to_all(back, ("zl", "head"), 0, 0)
    back = back.reshape(2, n_head, 2, 2, granule, 2 * head_dim)
    back = back.transpose(3, 0, 2, 4, 1, 5).reshape(row_count, n_head * 2 * head_dim)

    product_place = jnp.stack([head, quarter, quarter ^ 1, quarter ^ 2, quarter ^ 3])
    input_grad = run_product(product_place.astype(jnp.int32), back, key_own, value_own, weights)

    dq = dq.reshape(2, 2 * row_count, groups * head_dim)
    dq = dq[0] + lax.ppermute(dq[1].astype(bf16), "zl", swap).astype(f32)
    query_grad = dq[:row_count] + lax.ppermute(dq[row_count:], "core", swap)
    return (input_grad, query_grad.astype(bf16))


def solution(mesh):
    ctx = ("x", "zl", "y", "core")
    split = Mesh(mesh.devices.reshape(4, 2, 4, 2, n_head), ctx + ("head",))
    return jax.shard_map(
        shards,
        mesh=split,
        in_specs=(
            P(ctx, None),
            P(None, "head"),
            P(None, "head"),
            P(ctx, "head"),
            P(ctx, "head"),
            P(ctx),
            P(),
        ),
        out_specs=(P(ctx, "head"), P(ctx, "head")),
        check_vma=False,
    )
```

```python
import functools
import math

import jax
import jax.numpy as jnp
from jax import lax
from jax.experimental import pallas as pl
from jax.experimental.pallas import tpu as pltpu
from jax.sharding import Mesh
from jax.sharding import PartitionSpec as P

rope_base = 500000.0
big_negative = -1e30
n_ctx = 64
n_head = 4
block_len = 64
key_span = 256
granule = 16
log2e = 1.4426950408889634


swap = [(0, 1), (1, 0)]
both_swap = [(0, 3), (1, 2), (2, 1), (3, 0)]


def head_perm(s):
    return [(h, (h + s) % n_head) for h in range(n_head)]


def rotation_tables(positions, width):
    half_width = width // 2
    exponent = jnp.arange(half_width, dtype=jnp.float32) * (2.0 / width)
    frequency = jnp.exp(-math.log(rope_base) * exponent)
    angles = positions.astype(jnp.float32)[:, None] * frequency[None, :]
    return (jnp.cos(angles), jnp.sin(angles))


def rotate(vectors, cos_table, sin_table):
    half_width = vectors.shape[1] // 2
    a = vectors[:, :half_width]
    b = vectors[:, half_width:]
    return jnp.concatenate([a * cos_table - b * sin_table, b * cos_table + a * sin_table], axis=1)


def stored_block(place_ref, x, y, rel, block):
    z_at = place_ref[2] ^ (rel // 2)
    core_at = place_ref[3] ^ (rel % 2)
    return ((x * 2 + z_at) * 4 + y) * 4 + core_at * 2 + block


def each_granule(place_ref, order_ref, visit):
    def one_node(node, carry):
        for rel in range(4):
            for block in range(2):
                stored = stored_block(place_ref, node // 4, node % 4, rel, block)
                visit(order_ref[stored], node * 8 + rel * 2 + block)
        return carry

    lax.fori_loop(0, 16, one_node, 0, unroll=2)


def granule_rows(index):
    return pl.ds(pl.multiple_of(index * granule, granule), granule)


def load_operands(place_ref, order_ref, gathered, packs, kv, q_rows, g_rows, starts):
    tokens = kv.shape[0] - key_span
    kv[tokens:, :] = jnp.zeros_like(kv[tokens:, :])

    def fetch(seq, entry):
        kv[granule_rows(seq), :] = gathered[granule_rows(entry), :]

    each_granule(place_ref, order_ref, fetch)
    head_dim = q_rows.shape[1]
    half = starts.shape[1]
    for rel in range(4):
        pack = packs[rel]
        code = pack[256:272, :].astype(jnp.float32)
        start = (code[0:1, :] * 128.0 + code[1:2, :]).astype(jnp.int32)
        for block in range(2):
            part = rel * 2 + block
            starts[part : part + 1, :] = start[:, block * half : (block + 1) * half]
            for group in range(half // block_len):
                to = pl.ds(part * half + group * block_len, block_len)
                cols = pl.ds(group * head_dim, head_dim)
                q_rows[to, :] = pack[block * block_len : (block + 1) * block_len, cols]
                g_rows[to, :] = pack[128 + block * block_len : 128 + (block + 1) * block_len, cols]


def query_part(place_ref, order_ref, part, start):
    half = start.shape[1]
    rel = part // 2
    block = order_ref[stored_block(place_ref, place_ref[0], place_ref[1], rel, part % 2)]
    first_block = jnp.min(start) // block_len
    tiles = ((block - first_block + 1) * granule + key_span - 1) // key_span
    lane = lax.broadcasted_iota(jnp.int32, (1, half), 1)
    slot = ((place_ref[2] * 2 + place_ref[3]) ^ rel) * 2 + part % 2
    return first_block, tiles, slot, block * block_len + lane % block_len


chunk = 512
contract_last = (((1,), (1,)), ((), ()))


def tile_rows(kt, first_block, place_ref):
    base = first_block * granule + kt * key_span
    quarter = place_ref[2] * 2 + place_ref[3]
    offset = (first_block + kt * (key_span // granule)) * block_len + quarter * granule
    return pl.ds(pl.multiple_of(base, granule), key_span), offset


def fill_positions(key_rel):
    row = lax.broadcasted_iota(jnp.int32, key_rel.shape, 0)
    key_rel[...] = (row // granule) * block_len + row % granule


def chunk_terms(key, value, q_wide, g_part, pos, start, key_rel, factor):
    score = lax.dot_general(key, q_wide, contract_last, preferred_element_type=jnp.float32) * factor
    prob_grad = lax.dot_general(value, g_part, contract_last, preferred_element_type=jnp.float32)
    live = (key_rel <= pos) & (key_rel >= start)
    return score, prob_grad, live


def stats_kernel(place_ref, order_ref, *refs, factor):
    gathered, packs, stats_ref = refs[0], refs[1:5], refs[5]
    kv, q_rows, g_rows, starts, key_rel = refs[6:]
    load_operands(place_ref, order_ref, gathered, packs, kv, q_rows, g_rows, starts)
    half = starts.shape[1]
    head_dim = q_rows.shape[1]
    fill_positions(key_rel)

    def one_part(part, carry):
        start = starts[pl.ds(part, 1), :]
        first_block, tiles, slot, pos = query_part(place_ref, order_ref, part, start)

        def stats(kt, carried):
            rows, offset = tile_rows(kt, first_block, place_ref)
            key = kv[rows, : 2 * head_dim]
            value = kv[rows, 2 * head_dim :]
            result = []
            for c in range(half // chunk):
                top, total, weighted = carried[c]
                at = slice(c * chunk, (c + 1) * chunk)
                to = pl.ds(pl.multiple_of(part * half + c * chunk, chunk), chunk)
                q_part = q_rows[to, :]
                score, prob_grad, live = chunk_terms(
                    key,
                    value,
                    jnp.concatenate([q_part, q_part], axis=1),
                    g_rows[to, :],
                    pos[:, at] - offset,
                    start[:, at] - offset,
                    key_rel[...],
                    factor,
                )
                score = jnp.where(live, score, big_negative)
                new_top = jnp.maximum(top, jnp.max(score, axis=0, keepdims=True))
                growth = jnp.exp2(score - new_top)
                faded = jnp.exp2(top - new_top)
                result.append(
                    (
                        new_top,
                        total * faded + jnp.sum(growth, axis=0, keepdims=True),
                        weighted * faded + jnp.sum(growth * prob_grad, axis=0, keepdims=True),
                    )
                )
            return tuple(result)

        row = (1, chunk)
        zero = jnp.zeros(row, jnp.float32)
        init = (jnp.full(row, big_negative, jnp.float32), zero, zero)
        carried = lax.fori_loop(0, tiles, stats, (init,) * (half // chunk))
        top, total, weighted = (jnp.concatenate(v, axis=1) for v in zip(*carried))
        stats_ref[pl.ds(slot, 1), :] = top + jnp.log2(total)
        stats_ref[pl.ds(8 + slot, 1), :] = weighted / total
        return carry

    lax.fori_loop(0, 8, one_part, 0)


def grads_kernel(place_ref, order_ref, *refs, factor, scaling):
    gathered, packs, stats = refs[0], refs[1:5], refs[5:9]
    out_ref, dq_own, dq_others = refs[9], refs[10], refs[11:14]
    kv, q_rows, g_rows, starts, key_rel, acc, dq_acc, logs, deltas = refs[14:23]
    out_buf, own_buf, *other_bufs, sems = refs[23:]
    dq_bufs = (own_buf, *other_bufs)
    copies = [
        pltpu.make_async_copy(buf, ref, sems.at[i])
        for i, (buf, ref) in enumerate(zip((*dq_bufs, out_buf), (dq_own, *dq_others, out_ref)))
    ]
    load_operands(place_ref, order_ref, gathered, packs, kv, q_rows, g_rows, starts)
    half = starts.shape[1]
    head_dim = q_rows.shape[1]
    acc[...] = jnp.zeros_like(acc)
    fill_positions(key_rel)

    top = jnp.maximum(
        jnp.maximum(stats[0][:8, :], stats[1][:8, :]), jnp.maximum(stats[2][:8, :], stats[3][:8, :])
    )
    total = jnp.zeros_like(top)
    weighted = jnp.zeros_like(top)
    for s in stats:
        share = jnp.exp2(s[:8, :] - top)
        total = total + share
        weighted = weighted + share * s[8:, :]
    logs[...] = top + jnp.log2(total)
    deltas[...] = weighted / total

    def one_part(part, carry):
        start = starts[pl.ds(part, 1), :]
        first_block, tiles, slot, pos = query_part(place_ref, order_ref, part, start)
        log_total = logs[pl.ds(slot, 1), :]
        delta = deltas[pl.ds(slot, 1), :]
        dq_acc[...] = jnp.zeros_like(dq_acc)

        def grads(kt, carry):
            rows, offset = tile_rows(kt, first_block, place_ref)
            key = kv[rows, : 2 * head_dim]
            value = kv[rows, 2 * head_dim :]
            key_t = key.T
            key_sum = acc[rows, :head_dim]
            value_sum = acc[rows, head_dim:]
            for c in range(half // chunk):
                at = slice(c * chunk, (c + 1) * chunk)
                to = pl.ds(pl.multiple_of(part * half + c * chunk, chunk), chunk)
                q_part = q_rows[to, :]
                g_part = g_rows[to, :]
                score, prob_grad, live = chunk_terms(
                    key,
                    value,
                    jnp.concatenate([q_part, q_part], axis=1),
                    g_part,
                    pos[:, at] - offset,
                    start[:, at] - offset,
                    key_rel[...],
                    factor,
                )
                prob = jnp.where(live, jnp.exp2(score - log_total[:, at]), 0.0)
                score_grad = (prob * ((prob_grad - delta[:, at]) * scaling)).astype(jnp.bfloat16)
                key_sum += jnp.dot(score_grad, q_part, preferred_element_type=jnp.float32)
                value_sum += jnp.dot(
                    prob.astype(jnp.bfloat16), g_part, preferred_element_type=jnp.float32
                )
                dq_acc[:, at] += jnp.dot(key_t, score_grad, preferred_element_type=jnp.float32)
            acc[rows, :head_dim] = key_sum
            acc[rows, head_dim:] = value_sum
            return carry

        lax.fori_loop(0, tiles, grads, 0)
        dq = (dq_acc[:head_dim, :] + dq_acc[head_dim:, :]).T
        to = pl.ds(pl.multiple_of((part % 2) * block_len, block_len), block_len)
        for rel, ref in enumerate(dq_bufs):

            @pl.when(part // 2 == rel)
            def _(ref=ref):
                for group in range(half // block_len):
                    ref[to, group * head_dim : (group + 1) * head_dim] = dq[
                        group * block_len : (group + 1) * block_len, :
                    ].astype(ref.dtype)

            @pl.when(part == 2 * rel + 1)
            def _(rel=rel):
                copies[rel].start()

        return carry

    lax.fori_loop(0, 8, one_part, 0)

    def store(seq, entry):
        out_buf[granule_rows(entry), :] = acc[granule_rows(seq), :].astype(jnp.bfloat16)

    each_granule(place_ref, order_ref, store)
    copies[4].start()
    for copy in copies:
        copy.wait()


def kernel_scratch(quarter, head_dim, rows):
    half = rows // 2
    return [
        pltpu.VMEM((quarter + key_span, 3 * head_dim), jnp.bfloat16),
        pltpu.VMEM((4 * rows, head_dim), jnp.bfloat16),
        pltpu.VMEM((4 * rows, head_dim), jnp.bfloat16),
        pltpu.VMEM((8, half), jnp.int32),
        pltpu.VMEM((key_span, chunk), jnp.int32),
    ]


def run_stats(place, order, gathered, packs, scaling, tokens, head_dim, rows):
    smem = pl.BlockSpec(memory_space=pltpu.SMEM)
    vmem = pl.BlockSpec(memory_space=pltpu.VMEM)
    return pl.pallas_call(
        functools.partial(stats_kernel, factor=scaling * log2e),
        out_shape=jax.ShapeDtypeStruct((16, rows // 2), jnp.float32),
        in_specs=[smem, smem] + [vmem] * 5,
        out_specs=vmem,
        scratch_shapes=kernel_scratch(tokens // 4, head_dim, rows),
        compiler_params=pltpu.CompilerParams(vmem_limit_bytes=32 * 1024 * 1024),
        cost_estimate=pl.CostEstimate(
            flops=8 * rows * tokens * head_dim,
            bytes_accessed=4 * 1024 * 1024,
            transcendentals=rows * tokens // 2,
        ),
    )(place, order, gathered, *packs)


def run_grads(place, order, gathered, packs, stats, scaling, tokens, head_dim, rows):
    smem = pl.BlockSpec(memory_space=pltpu.SMEM)
    vmem = pl.BlockSpec(memory_space=pltpu.VMEM)
    quarter = tokens // 4
    half = rows // 2
    return pl.pallas_call(
        functools.partial(grads_kernel, factor=scaling * log2e, scaling=scaling),
        out_shape=[
            jax.ShapeDtypeStruct((quarter, 2 * head_dim), jnp.bfloat16),
            jax.ShapeDtypeStruct((2 * block_len, (half // block_len) * head_dim), jnp.float32),
        ]
        + [jax.ShapeDtypeStruct((2 * block_len, (half // block_len) * head_dim), jnp.bfloat16)] * 3,
        in_specs=[smem, smem] + [vmem] * 9,
        out_specs=[pl.BlockSpec(memory_space=pltpu.HBM)] * 5,
        scratch_shapes=kernel_scratch(quarter, head_dim, rows)
        + [
            pltpu.VMEM((quarter + key_span, 2 * head_dim), jnp.float32),
            pltpu.VMEM((2 * head_dim, half), jnp.float32),
            pltpu.VMEM((8, half), jnp.float32),
            pltpu.VMEM((8, half), jnp.float32),
            pltpu.VMEM((quarter, 2 * head_dim), jnp.bfloat16),
            pltpu.VMEM((2 * block_len, (half // block_len) * head_dim), jnp.float32),
        ]
        + [pltpu.VMEM((2 * block_len, (half // block_len) * head_dim), jnp.bfloat16)] * 3
        + [pltpu.SemaphoreType.DMA((5,))],
        compiler_params=pltpu.CompilerParams(vmem_limit_bytes=58 * 1024 * 1024),
        cost_estimate=pl.CostEstimate(
            flops=16 * rows * tokens * head_dim,
            bytes_accessed=8 * 1024 * 1024,
            transcendentals=rows * tokens // 2,
        ),
    )(place, order, gathered, *packs, *stats)


def finish_kernel(place_ref, parts_ref, cos_ref, sin_ref, out_ref):
    head_dim = cos_ref.shape[1]
    rows = out_ref.shape[1]
    for rel in range(4):
        at = pl.ds(rel * rows, rows)
        total = parts_ref[0, at, :].astype(jnp.float32)
        for i in range(1, parts_ref.shape[0]):
            total += parts_ref[i, at, :].astype(jnp.float32)
        key = total[:, :head_dim]
        key = key * cos_ref[at, :] + pltpu.roll(key, head_dim // 2, 1) * sin_ref[at, :]
        back = jnp.concatenate([key, total[:, head_dim:]], axis=1).astype(jnp.bfloat16)
        owner = (place_ref[0] ^ rel) * n_head
        for head in range(n_head):
            out_ref[owner + head] = back


def run_finish(place, parts, cos_wide, sin_wide):
    smem = pl.BlockSpec(memory_space=pltpu.SMEM)
    vmem = pl.BlockSpec(memory_space=pltpu.VMEM)
    _, rows, width = parts.shape
    return pl.pallas_call(
        finish_kernel,
        out_shape=jax.ShapeDtypeStruct((4 * n_head, rows // 4, width), jnp.bfloat16),
        in_specs=[smem] + [vmem] * 3,
        out_specs=vmem,
        compiler_params=pltpu.CompilerParams(vmem_limit_bytes=16 * 1024 * 1024),
        cost_estimate=pl.CostEstimate(
            flops=20 * rows * width, bytes_accessed=2 * 1024 * 1024, transcendentals=0
        ),
    )(place, parts, cos_wide, sin_wide)


def product_kernel(place_ref, back_ref, mine_ref, other_ref, out_ref, left_mine, left_other):
    head_dim = back_ref.shape[2] // 2
    first = pl.multiple_of(place_ref[1] * head_dim, head_dim)
    second = pl.multiple_of(head_dim - first, head_dim)
    for source in range(back_ref.shape[0]):
        quarter, shift = source // n_head, source % n_head
        sender = quarter * n_head + (place_ref[2] + n_head - shift) % n_head
        cols = pl.ds(shift * head_dim, head_dim)
        for block in range(2):
            to = pl.ds(block * block_len + quarter * granule, granule)
            at = pl.ds(block * granule, granule)
            left_mine[to, cols] = back_ref[sender, at, pl.ds(first, head_dim)]
            left_other[to, cols] = back_ref[sender, at, pl.ds(second, head_dim)]
    for tile in range(out_ref.shape[1] // 512):
        at = pl.ds(tile * 512, 512)
        total = lax.dot_general(
            left_mine[...], mine_ref[at, :], contract_last, preferred_element_type=jnp.float32
        )
        total += lax.dot_general(
            left_other[...], other_ref[at, :], contract_last, preferred_element_type=jnp.float32
        )
        out_ref[:, at] = total.astype(jnp.bfloat16)


def run_product(place, back, mine, other):
    smem = pl.BlockSpec(memory_space=pltpu.SMEM)
    vmem = pl.BlockSpec(memory_space=pltpu.VMEM)
    row_count = back.shape[0] * back.shape[1] // n_head
    out_width, depth = mine.shape
    return pl.pallas_call(
        product_kernel,
        out_shape=jax.ShapeDtypeStruct((row_count, out_width), jnp.bfloat16),
        in_specs=[smem] + [vmem] * 3,
        out_specs=vmem,
        scratch_shapes=[pltpu.VMEM((row_count, depth), jnp.bfloat16)] * 2,
        compiler_params=pltpu.CompilerParams(vmem_limit_bytes=24 * 1024 * 1024),
        cost_estimate=pl.CostEstimate(
            flops=4 * row_count * depth * out_width,
            bytes_accessed=5 * 1024 * 1024,
            transcendentals=0,
        ),
    )(place, back, mine, other)


def shards(layer_input, key_weight, value_weight, queries, out_grad, doc_start, block_order):
    f32, bf16 = jnp.float32, jnp.bfloat16
    row_count = layer_input.shape[0]
    tokens = row_count * n_ctx
    head_dim = key_weight.shape[1]
    width = key_weight.shape[0]
    groups = queries.shape[1] // head_dim
    rows = row_count * groups
    scaling = 1.0 / math.sqrt(head_dim)
    x, y = lax.axis_index("x"), lax.axis_index("y")
    z, core, head = lax.axis_index("zl"), lax.axis_index("core"), lax.axis_index("head")
    core_is_one = core == 1

    def pick(v, index, axis):
        return lax.dynamic_index_in_dim(v, index, axis, keepdims=False)

    def blocks_of(z_at, core_at):
        at = ((x * 2 + z_at) * 4 + y) * 4 + core_at * 2
        return lax.dynamic_slice_in_dim(block_order, at, 2)

    own_blocks = blocks_of(z, core)
    own_pos = (
        own_blocks[:, None] * block_len + jnp.arange(block_len, dtype=jnp.int32)[None, :]
    ).reshape(-1)
    cos_own, sin_own = rotation_tables(own_pos, head_dim)
    key_raw = jnp.dot(layer_input, key_weight, preferred_element_type=f32)
    keys = rotate(key_raw, cos_own, sin_own)
    key_hi = lax.reduce_precision(keys, 8, 7)
    key_lo = keys - key_hi
    values = jnp.dot(layer_input, value_weight, preferred_element_type=f32)
    local = jnp.concatenate(
        [key_hi.astype(bf16), key_lo.astype(bf16), values.astype(bf16)], axis=1
    ).reshape(2, 2, 2, granule, 3 * head_dim)

    pair = jnp.stack(
        [pick(local, core, 2), lax.ppermute(pick(local, 1 - core, 2), "core", swap)]
    )

    out_width = width // n_head
    share = out_width // 16
    node_index = x * 4 + y

    def weight_share(w):
        return pick(w.reshape(n_head, 16, share, head_dim), node_index, 1)

    weight_shares = jnp.where(
        core_is_one, weight_share(value_weight), weight_share(key_weight)
    )
    pair, weight_shares = lax.optimization_barrier((pair, weight_shares))
    weight_rows = [pick(weight_shares, head, 0)] + [
        lax.ppermute(pick(weight_shares, (head + s) % n_head, 0), "head", head_perm(s))
        for s in (1, 2, 3)
    ]
    weight_rows = jnp.concatenate(weight_rows, axis=1)[None]

    def per_column(v):
        return jnp.broadcast_to(v.reshape(2, 1, block_len), (2, groups, block_len)).reshape(1, rows)

    start_cols = per_column(doc_start)
    start_code = jnp.concatenate(
        [start_cols // 128, start_cols % 128, jnp.zeros((14, rows), jnp.int32)], axis=0
    ).astype(bf16)
    pack_own = jnp.concatenate([queries, out_grad, start_code], axis=0)
    node = jnp.stack([pick(pair, z, 2), lax.ppermute(pick(pair, 1 - z, 2), "zl", swap)])
    node = node.reshape(1, row_count, 3 * head_dim)
    pack_z = lax.ppermute(pack_own, "zl", swap)
    pack_z, weight_rows = lax.optimization_barrier((pack_z, weight_rows))
    packs = [
        pack_own,
        lax.ppermute(pack_own, "core", swap),
        pack_z,
        lax.ppermute(pack_z, "core", swap),
    ]

    gathered = lax.all_to_all(
        jnp.broadcast_to(node, (16, row_count, 3 * head_dim)), ("x", "y"), 0, 0
    ).reshape(tokens // 4, 3 * head_dim)
    weights_mine = lax.all_to_all(
        jnp.broadcast_to(weight_rows, (16, share, n_head * head_dim)), ("x", "y"), 0, 0
    )

    quarter = z * 2 + core
    place = jnp.stack([x, y, z, core]).astype(jnp.int32)
    stats = run_stats(place, block_order, gathered, packs, scaling, tokens, head_dim, rows)
    stats_all = [
        stats,
        lax.ppermute(stats, "core", swap),
        lax.ppermute(stats, "zl", swap),
        lax.ppermute(stats, ("zl", "core"), both_swap),
    ]
    grads, dq_own, *dq_others = run_grads(
        place, block_order, gathered, packs, stats_all, scaling, tokens, head_dim, rows
    )
    grads, weights_mine = lax.optimization_barrier((grads, weights_mine))
    weights_mine = weights_mine.reshape(out_width, n_head * head_dim)
    weights_other = lax.ppermute(weights_mine, "core", swap)

    grads = lax.all_to_all(
        grads.reshape(16, row_count, 2 * head_dim), ("x", "y"), 0, 0
    )
    node_blocks = jnp.concatenate(
        [blocks_of(z ^ (rel // 2), core ^ (rel % 2)) for rel in range(4)]
    )
    quarter_pos = (
        node_blocks[:, None] * block_len
        + quarter * granule
        + jnp.arange(granule, dtype=jnp.int32)[None, :]
    ).reshape(-1)
    cos_node, sin_node = rotation_tables(quarter_pos, head_dim)

    here = jnp.stack([quarter, core, head]).astype(jnp.int32)
    back = run_finish(
        here,
        grads,
        jnp.concatenate([cos_node, cos_node], axis=1),
        jnp.concatenate([sin_node, -sin_node], axis=1),
    )
    back = lax.all_to_all(back, ("zl", "core", "head"), 0, 0)
    input_grad = run_product(here, back, weights_mine, weights_other)

    dq_sum = (
        dq_own
        + lax.ppermute(dq_others[0], "core", swap).astype(f32)
        + lax.ppermute(dq_others[1], "zl", swap).astype(f32)
        + lax.ppermute(dq_others[2], ("zl", "core"), both_swap).astype(f32)
    )
    return (input_grad, dq_sum.astype(bf16))


def solution(mesh):
    ctx = ("x", "zl", "y", "core")
    split = Mesh(mesh.devices.reshape(4, 2, 4, 2, n_head), ctx + ("head",))
    return jax.shard_map(
        shards,
        mesh=split,
        in_specs=(
            P(ctx, None),
            P(None, "head"),
            P(None, "head"),
            P(ctx, "head"),
            P(ctx, "head"),
            P(ctx),
            P(),
        ),
        out_specs=(P(ctx, "head"), P(ctx, "head")),
        check_vma=False,
    )
```

```python
import functools
import math

import jax
import jax.numpy as jnp
from jax import lax
from jax.experimental import pallas as pl
from jax.experimental.pallas import tpu as pltpu
from jax.sharding import Mesh
from jax.sharding import PartitionSpec as P

rope_base = 500000.0
big_negative = -1e30
n_ctx = 64
n_head = 4
block_len = 64
key_span = 256
granule = 16
item_group = 3
log2e = 1.4426950408889634


swap = [(0, 1), (1, 0)]
both_swap = [(0, 3), (1, 2), (2, 1), (3, 0)]


def head_perm(s):
    return [(h, (h + s) % n_head) for h in range(n_head)]


def rotation_tables(positions, width):
    half_width = width // 2
    exponent = jnp.arange(half_width, dtype=jnp.float32) * (2.0 / width)
    frequency = jnp.exp(-math.log(rope_base) * exponent)
    angles = positions.astype(jnp.float32)[:, None] * frequency[None, :]
    return (jnp.cos(angles), jnp.sin(angles))


def rotate(vectors, cos_table, sin_table):
    half_width = vectors.shape[1] // 2
    a = vectors[:, :half_width]
    b = vectors[:, half_width:]
    return jnp.concatenate([a * cos_table - b * sin_table, b * cos_table + a * sin_table], axis=1)


def stored_block(place_ref, x, y, rel, block):
    z_at = place_ref[2] ^ (rel // 2)
    core_at = place_ref[3] ^ (rel % 2)
    return ((x * 2 + z_at) * 4 + y) * 4 + core_at * 2 + block


def each_granule(place_ref, order_ref, visit):
    def one_node(node, carry):
        for rel in range(4):
            for block in range(2):
                stored = stored_block(place_ref, node // 4, node % 4, rel, block)
                visit(order_ref[stored], node * 8 + rel * 2 + block)
        return carry

    lax.fori_loop(0, 16, one_node, 0, unroll=2)


def granule_rows(index):
    return pl.ds(pl.multiple_of(index * granule, granule), granule)


def load_operands(place_ref, order_ref, gathered, packs, kv, q_rows, g_rows, starts):
    tokens = kv.shape[0] - key_span
    kv[tokens:, :] = jnp.zeros_like(kv[tokens:, :])

    def fetch(seq, entry):
        kv[granule_rows(seq), :] = gathered[granule_rows(entry), :]

    each_granule(place_ref, order_ref, fetch)
    head_dim = q_rows.shape[1]
    half = starts.shape[1]
    for rel in range(4):
        pack = packs[rel]
        code = pack[256:272, :].astype(jnp.float32)
        start = (code[0:1, :] * 128.0 + code[1:2, :]).astype(jnp.int32)
        for block in range(2):
            part = rel * 2 + block
            starts[part : part + 1, :] = start[:, block * half : (block + 1) * half]
            for group in range(half // block_len):
                to = pl.ds(part * half + group * block_len, block_len)
                cols = pl.ds(group * head_dim, head_dim)
                q_rows[to, :] = pack[block * block_len : (block + 1) * block_len, cols]
                g_rows[to, :] = pack[128 + block * block_len : 128 + (block + 1) * block_len, cols]


contract_last = (((1,), (1,)), ((), ()))


def part_block(place_ref, order_ref, part):
    return order_ref[stored_block(place_ref, place_ref[0], place_ref[1], part // 2, part % 2)]


def part_slot(place_ref, part):
    return ((place_ref[2] * 2 + place_ref[3]) ^ (part // 2)) * 2 + part % 2


def list_items(place_ref, order_ref, starts, items):
    filled = 0
    for part in range(8):
        block = part_block(place_ref, order_ref, part)
        first = jnp.min(starts[part : part + 1, :]) // block_len
        count = (block - first + key_span // granule) // (key_span // granule)

        def add(k, at, part=part, block=block, first=first):
            items[0, at] = part
            items[1, at] = first + k * (key_span // granule)
            items[2, at] = block * block_len
            return at + 1

        filled = lax.fori_loop(0, count, add, filled)
    for spare in range(item_group - 1):
        items[0, filled + spare] = 7
        items[1, filled + spare] = 16 * 8
        items[2, filled + spare] = 0
    return (filled + item_group - 1) // item_group


def fill_positions(key_rel):
    row = lax.broadcasted_iota(jnp.int32, key_rel.shape, 0)
    key_rel[...] = (row // granule) * block_len + row % granule


def item_terms(i, items, place_ref, kv, q_rows, g_rows, starts, key_rel, factor):
    part, first = items[0, i], items[1, i]
    half = starts.shape[1]
    head_dim = q_rows.shape[1]
    rows = pl.ds(pl.multiple_of(first * granule, granule), key_span)
    cols = pl.ds(pl.multiple_of(part * half, half), half)
    offset = first * block_len + (place_ref[2] * 2 + place_ref[3]) * granule
    key = kv[rows, : 2 * head_dim]
    value = kv[rows, 2 * head_dim :]
    q_part = q_rows[cols, :]
    g_part = g_rows[cols, :]
    score = lax.dot_general(
        key,
        jnp.concatenate([q_part, q_part], axis=1),
        contract_last,
        preferred_element_type=jnp.float32,
    )
    prob_grad = lax.dot_general(value, g_part, contract_last, preferred_element_type=jnp.float32)
    lane = lax.broadcasted_iota(jnp.int32, (1, half), 1) % block_len
    end = lane + (items[2, i] - offset)
    start = starts[pl.ds(part, 1), :] - offset
    live = (key_rel[...] <= end) & (key_rel[...] >= start)
    return part, rows, key, q_part, g_part, score * factor, prob_grad, live


def stats_kernel(place_ref, order_ref, *refs, factor):
    gathered, packs, stats_ref = refs[0], refs[1:5], refs[5]
    kv, q_rows, g_rows, starts, key_rel, items, tops, totals, weights = refs[6:]
    load_operands(place_ref, order_ref, gathered, packs, kv, q_rows, g_rows, starts)
    fill_positions(key_rel)
    tops[...] = jnp.full_like(tops, big_negative)
    totals[...] = jnp.zeros_like(totals)
    weights[...] = jnp.zeros_like(weights)
    step_count = list_items(place_ref, order_ref, starts, items)

    def one_step(step, carry):
        both = [
            item_terms(
                item_group * step + i, items, place_ref, kv, q_rows, g_rows, starts, key_rel, factor
            )
            for i in range(item_group)
        ]
        for part, _, _, _, _, score, prob_grad, live in both:
            at = pl.ds(part, 1)
            top = tops[at, :]
            score = jnp.where(live, score, big_negative)
            new_top = jnp.maximum(top, jnp.max(score, axis=0, keepdims=True))
            growth = jnp.exp2(score - new_top)
            faded = jnp.exp2(top - new_top)
            tops[at, :] = new_top
            totals[at, :] = totals[at, :] * faded + jnp.sum(growth, axis=0, keepdims=True)
            weights[at, :] = weights[at, :] * faded + jnp.sum(
                growth * prob_grad, axis=0, keepdims=True
            )
        return carry

    lax.fori_loop(0, step_count, one_step, 0)
    for part in range(8):
        slot = part_slot(place_ref, part)
        at = slice(part, part + 1)
        stats_ref[pl.ds(slot, 1), :] = tops[at, :] + jnp.log2(totals[at, :])
        stats_ref[pl.ds(8 + slot, 1), :] = weights[at, :] / totals[at, :]


def grads_kernel(place_ref, order_ref, *refs, factor, scaling):
    gathered, packs, stats = refs[0], refs[1:5], refs[5:9]
    out_ref, dq_own, dq_others = refs[9], refs[10], refs[11:14]
    kv, q_rows, g_rows, starts, key_rel, items, acc, dq_acc, logs, deltas = refs[14:24]
    out_buf, own_buf, *other_bufs, sems = refs[24:]
    dq_bufs = (own_buf, *other_bufs)
    copies = [
        pltpu.make_async_copy(buf, ref, sems.at[i])
        for i, (buf, ref) in enumerate(zip((*dq_bufs, out_buf), (dq_own, *dq_others, out_ref)))
    ]
    load_operands(place_ref, order_ref, gathered, packs, kv, q_rows, g_rows, starts)
    half = starts.shape[1]
    head_dim = q_rows.shape[1]
    acc[...] = jnp.zeros_like(acc)
    fill_positions(key_rel)

    top = jnp.maximum(
        jnp.maximum(stats[0][:8, :], stats[1][:8, :]), jnp.maximum(stats[2][:8, :], stats[3][:8, :])
    )
    total = jnp.zeros_like(top)
    weighted = jnp.zeros_like(top)
    for s in stats:
        share = jnp.exp2(s[:8, :] - top)
        total = total + share
        weighted = weighted + share * s[8:, :]
    logs[...] = top + jnp.log2(total)
    deltas[...] = weighted / total

    dq_acc[...] = jnp.zeros_like(dq_acc)
    step_count = list_items(place_ref, order_ref, starts, items)
    quarter = place_ref[2] * 2 + place_ref[3]

    def one_step(step, carry):
        both = [
            item_terms(
                item_group * step + i, items, place_ref, kv, q_rows, g_rows, starts, key_rel, factor
            )
            for i in range(item_group)
        ]
        results = []
        for part, rows, key, q_part, g_part, score, prob_grad, live in both:
            slot = pl.ds((quarter ^ (part // 2)) * 2 + part % 2, 1)
            prob = jnp.where(live, jnp.exp2(score - logs[slot, :]), 0.0)
            score_grad = (prob * ((prob_grad - deltas[slot, :]) * scaling)).astype(jnp.bfloat16)
            key_part = jnp.dot(score_grad, q_part, preferred_element_type=jnp.float32)
            value_part = jnp.dot(
                prob.astype(jnp.bfloat16), g_part, preferred_element_type=jnp.float32
            )
            query_part = jnp.dot(key.T, score_grad, preferred_element_type=jnp.float32)
            results.append((part, rows, key_part, value_part, query_part))
        for part, rows, key_part, value_part, query_part in results:
            acc[rows, :head_dim] += key_part
            acc[rows, head_dim:] += value_part
            at = pl.ds(pl.multiple_of(part * head_dim, head_dim), head_dim)
            dq_acc[at, :] += query_part[:head_dim, :] + query_part[head_dim:, :]
        return carry

    lax.fori_loop(0, step_count, one_step, 0)
    for part in range(8):
        dq = dq_acc[part * head_dim : (part + 1) * head_dim, :].T
        rel, block = part // 2, part % 2
        buf = dq_bufs[rel]
        for group in range(half // block_len):
            buf[block * block_len : (block + 1) * block_len, pl.ds(group * head_dim, head_dim)] = (
                dq[group * block_len : (group + 1) * block_len, :].astype(buf.dtype)
            )
        if block == 1:
            copies[rel].start()

    def store(seq, entry):
        out_buf[granule_rows(entry), :] = acc[granule_rows(seq), :].astype(jnp.bfloat16)

    each_granule(place_ref, order_ref, store)
    copies[4].start()
    for copy in copies:
        copy.wait()


def kernel_scratch(quarter, head_dim, rows):
    half = rows // 2
    return [
        pltpu.VMEM((quarter + key_span, 3 * head_dim), jnp.bfloat16),
        pltpu.VMEM((4 * rows, head_dim), jnp.bfloat16),
        pltpu.VMEM((4 * rows, head_dim), jnp.bfloat16),
        pltpu.VMEM((8, half), jnp.int32),
        pltpu.VMEM((key_span, half), jnp.int32),
        pltpu.SMEM((3, 64), jnp.int32),
    ]


def run_stats(place, order, gathered, packs, scaling, tokens, head_dim, rows):
    smem = pl.BlockSpec(memory_space=pltpu.SMEM)
    vmem = pl.BlockSpec(memory_space=pltpu.VMEM)
    return pl.pallas_call(
        functools.partial(stats_kernel, factor=scaling * log2e),
        out_shape=jax.ShapeDtypeStruct((16, rows // 2), jnp.float32),
        in_specs=[smem, smem] + [vmem] * 5,
        out_specs=vmem,
        scratch_shapes=kernel_scratch(tokens // 4, head_dim, rows)
        + [pltpu.VMEM((8, rows // 2), jnp.float32)] * 3,
        compiler_params=pltpu.CompilerParams(vmem_limit_bytes=32 * 1024 * 1024),
        cost_estimate=pl.CostEstimate(
            flops=8 * rows * tokens * head_dim,
            bytes_accessed=4 * 1024 * 1024,
            transcendentals=rows * tokens // 2,
        ),
    )(place, order, gathered, *packs)


def run_grads(place, order, gathered, packs, stats, scaling, tokens, head_dim, rows):
    smem = pl.BlockSpec(memory_space=pltpu.SMEM)
    vmem = pl.BlockSpec(memory_space=pltpu.VMEM)
    quarter = tokens // 4
    half = rows // 2
    return pl.pallas_call(
        functools.partial(grads_kernel, factor=scaling * log2e, scaling=scaling),
        out_shape=[
            jax.ShapeDtypeStruct((quarter, 2 * head_dim), jnp.bfloat16),
            jax.ShapeDtypeStruct((2 * block_len, (half // block_len) * head_dim), jnp.float32),
        ]
        + [jax.ShapeDtypeStruct((2 * block_len, (half // block_len) * head_dim), jnp.bfloat16)] * 3,
        in_specs=[smem, smem] + [vmem] * 9,
        out_specs=[pl.BlockSpec(memory_space=pltpu.HBM)] * 5,
        scratch_shapes=kernel_scratch(quarter, head_dim, rows)
        + [
            pltpu.VMEM((quarter + key_span, 2 * head_dim), jnp.float32),
            pltpu.VMEM((8 * head_dim, half), jnp.float32),
            pltpu.VMEM((8, half), jnp.float32),
            pltpu.VMEM((8, half), jnp.float32),
            pltpu.VMEM((quarter, 2 * head_dim), jnp.bfloat16),
            pltpu.VMEM((2 * block_len, (half // block_len) * head_dim), jnp.float32),
        ]
        + [pltpu.VMEM((2 * block_len, (half // block_len) * head_dim), jnp.bfloat16)] * 3
        + [pltpu.SemaphoreType.DMA((5,))],
        compiler_params=pltpu.CompilerParams(vmem_limit_bytes=57 * 1024 * 1024),
        cost_estimate=pl.CostEstimate(
            flops=16 * rows * tokens * head_dim,
            bytes_accessed=8 * 1024 * 1024,
            transcendentals=rows * tokens // 2,
        ),
    )(place, order, gathered, *packs, *stats)


def finish_kernel(place_ref, parts_ref, cos_ref, sin_ref, out_ref):
    head_dim = cos_ref.shape[1]
    rows = out_ref.shape[1]
    for rel in range(4):
        at = pl.ds(rel * rows, rows)
        total = parts_ref[0, at, :].astype(jnp.float32)
        for i in range(1, parts_ref.shape[0]):
            total += parts_ref[i, at, :].astype(jnp.float32)
        key = total[:, :head_dim]
        key = key * cos_ref[at, :] + pltpu.roll(key, head_dim // 2, 1) * sin_ref[at, :]
        back = jnp.concatenate([key, total[:, head_dim:]], axis=1).astype(jnp.bfloat16)
        owner = (place_ref[0] ^ rel) * n_head
        for head in range(n_head):
            out_ref[owner + head] = back


def run_finish(place, parts, cos_wide, sin_wide):
    smem = pl.BlockSpec(memory_space=pltpu.SMEM)
    vmem = pl.BlockSpec(memory_space=pltpu.VMEM)
    _, rows, width = parts.shape
    return pl.pallas_call(
        finish_kernel,
        out_shape=jax.ShapeDtypeStruct((4 * n_head, rows // 4, width), jnp.bfloat16),
        in_specs=[smem] + [vmem] * 3,
        out_specs=vmem,
        compiler_params=pltpu.CompilerParams(vmem_limit_bytes=16 * 1024 * 1024),
        cost_estimate=pl.CostEstimate(
            flops=20 * rows * width, bytes_accessed=2 * 1024 * 1024, transcendentals=0
        ),
    )(place, parts, cos_wide, sin_wide)


def product_kernel(place_ref, back_ref, mine_ref, other_ref, out_ref, left_mine, left_other):
    head_dim = back_ref.shape[2] // 2
    first = pl.multiple_of(place_ref[1] * head_dim, head_dim)
    second = pl.multiple_of(head_dim - first, head_dim)
    for source in range(back_ref.shape[0]):
        quarter, shift = source // n_head, source % n_head
        sender = quarter * n_head + (place_ref[2] + n_head - shift) % n_head
        cols = pl.ds(shift * head_dim, head_dim)
        for block in range(2):
            to = pl.ds(block * block_len + quarter * granule, granule)
            at = pl.ds(block * granule, granule)
            left_mine[to, cols] = back_ref[sender, at, pl.ds(first, head_dim)]
            left_other[to, cols] = back_ref[sender, at, pl.ds(second, head_dim)]
    for tile in range(out_ref.shape[1] // 512):
        at = pl.ds(tile * 512, 512)
        total = lax.dot_general(
            left_mine[...], mine_ref[at, :], contract_last, preferred_element_type=jnp.float32
        )
        total += lax.dot_general(
            left_other[...], other_ref[at, :], contract_last, preferred_element_type=jnp.float32
        )
        out_ref[:, at] = total.astype(jnp.bfloat16)


def run_product(place, back, mine, other):
    smem = pl.BlockSpec(memory_space=pltpu.SMEM)
    vmem = pl.BlockSpec(memory_space=pltpu.VMEM)
    row_count = back.shape[0] * back.shape[1] // n_head
    out_width, depth = mine.shape
    return pl.pallas_call(
        product_kernel,
        out_shape=jax.ShapeDtypeStruct((row_count, out_width), jnp.bfloat16),
        in_specs=[smem] + [vmem] * 3,
        out_specs=vmem,
        scratch_shapes=[pltpu.VMEM((row_count, depth), jnp.bfloat16)] * 2,
        compiler_params=pltpu.CompilerParams(vmem_limit_bytes=24 * 1024 * 1024),
        cost_estimate=pl.CostEstimate(
            flops=4 * row_count * depth * out_width,
            bytes_accessed=5 * 1024 * 1024,
            transcendentals=0,
        ),
    )(place, back, mine, other)


def shards(layer_input, key_weight, value_weight, queries, out_grad, doc_start, block_order):
    f32, bf16 = jnp.float32, jnp.bfloat16
    row_count = layer_input.shape[0]
    tokens = row_count * n_ctx
    head_dim = key_weight.shape[1]
    width = key_weight.shape[0]
    groups = queries.shape[1] // head_dim
    rows = row_count * groups
    scaling = 1.0 / math.sqrt(head_dim)
    x, y = lax.axis_index("x"), lax.axis_index("y")
    z, core, head = lax.axis_index("zl"), lax.axis_index("core"), lax.axis_index("head")
    core_is_one = core == 1

    def pick(v, index, axis):
        return lax.dynamic_index_in_dim(v, index, axis, keepdims=False)

    def blocks_of(z_at, core_at):
        at = ((x * 2 + z_at) * 4 + y) * 4 + core_at * 2
        return lax.dynamic_slice_in_dim(block_order, at, 2)

    own_blocks = blocks_of(z, core)
    own_pos = (
        own_blocks[:, None] * block_len + jnp.arange(block_len, dtype=jnp.int32)[None, :]
    ).reshape(-1)
    cos_own, sin_own = rotation_tables(own_pos, head_dim)
    key_raw = jnp.dot(layer_input, key_weight, preferred_element_type=f32)
    keys = rotate(key_raw, cos_own, sin_own)
    key_hi = lax.reduce_precision(keys, 8, 7)
    key_lo = keys - key_hi
    values = jnp.dot(layer_input, value_weight, preferred_element_type=f32)
    local = jnp.concatenate(
        [key_hi.astype(bf16), key_lo.astype(bf16), values.astype(bf16)], axis=1
    ).reshape(2, 2, 2, granule, 3 * head_dim)

    pair = jnp.stack(
        [pick(local, core, 2), lax.ppermute(pick(local, 1 - core, 2), "core", swap)]
    )

    node = jnp.stack([pick(pair, z, 2), lax.ppermute(pick(pair, 1 - z, 2), "zl", swap)])
    node = node.reshape(1, row_count, 3 * head_dim)

    out_width = width // n_head
    share = out_width // 16
    node_index = x * 4 + y

    def weight_share(w):
        return pick(w.reshape(n_head, 16, share, head_dim), node_index, 1)

    weight_shares = jnp.where(
        core_is_one, weight_share(value_weight), weight_share(key_weight)
    )
    node, weight_shares = lax.optimization_barrier((node, weight_shares))
    weight_rows = [pick(weight_shares, head, 0)] + [
        lax.ppermute(pick(weight_shares, (head + s) % n_head, 0), "head", head_perm(s))
        for s in (1, 2, 3)
    ]
    weight_rows = jnp.concatenate(weight_rows, axis=1)[None]
    weight_rows = jnp.broadcast_to(weight_rows, (16, share, n_head * head_dim))

    def per_column(v):
        return jnp.broadcast_to(v.reshape(2, 1, block_len), (2, groups, block_len)).reshape(1, rows)

    start_cols = per_column(doc_start)
    start_code = jnp.concatenate(
        [start_cols // 128, start_cols % 128, jnp.zeros((14, rows), jnp.int32)], axis=0
    ).astype(bf16)
    pack_own = jnp.concatenate([queries, out_grad, start_code], axis=0)
    pack_z = lax.ppermute(pack_own, "zl", swap)
    pack_z, weight_rows = lax.optimization_barrier((pack_z, weight_rows))
    packs = [
        pack_own,
        lax.ppermute(pack_own, "core", swap),
        pack_z,
        lax.ppermute(pack_z, "core", swap),
    ]

    gathered = lax.all_to_all(
        jnp.broadcast_to(node, (16, row_count, 3 * head_dim)), ("x", "y"), 0, 0
    ).reshape(tokens // 4, 3 * head_dim)
    weights_mine = lax.all_to_all(weight_rows, ("x", "y"), 0, 0)

    quarter = z * 2 + core
    place = jnp.stack([x, y, z, core]).astype(jnp.int32)
    stats = run_stats(place, block_order, gathered, packs, scaling, tokens, head_dim, rows)
    stats_all = [
        stats,
        lax.ppermute(stats, "core", swap),
        lax.ppermute(stats, "zl", swap),
        lax.ppermute(stats, ("zl", "core"), both_swap),
    ]
    grads, dq_own, *dq_others = run_grads(
        place, block_order, gathered, packs, stats_all, scaling, tokens, head_dim, rows
    )
    grads, weights_mine = lax.optimization_barrier((grads, weights_mine))
    weights_mine = weights_mine.reshape(out_width, n_head * head_dim)
    weights_other = lax.ppermute(weights_mine, "core", swap)

    grads = lax.all_to_all(
        grads.reshape(16, row_count, 2 * head_dim), ("x", "y"), 0, 0
    )
    node_blocks = jnp.concatenate(
        [blocks_of(z ^ (rel // 2), core ^ (rel % 2)) for rel in range(4)]
    )
    quarter_pos = (
        node_blocks[:, None] * block_len
        + quarter * granule
        + jnp.arange(granule, dtype=jnp.int32)[None, :]
    ).reshape(-1)
    cos_node, sin_node = rotation_tables(quarter_pos, head_dim)

    here = jnp.stack([quarter, core, head]).astype(jnp.int32)
    back = run_finish(
        here,
        grads,
        jnp.concatenate([cos_node, cos_node], axis=1),
        jnp.concatenate([sin_node, -sin_node], axis=1),
    )
    back = lax.all_to_all(back, ("zl", "core", "head"), 0, 0)
    input_grad = run_product(here, back, weights_mine, weights_other)

    dq_sum = (
        dq_own
        + lax.ppermute(dq_others[0], "core", swap).astype(f32)
        + lax.ppermute(dq_others[1], "zl", swap).astype(f32)
        + lax.ppermute(dq_others[2], ("zl", "core"), both_swap).astype(f32)
    )
    return (input_grad, dq_sum.astype(bf16))


def solution(mesh):
    ctx = ("x", "zl", "y", "core")
    split = Mesh(mesh.devices.reshape(4, 2, 4, 2, n_head), ctx + ("head",))
    return jax.shard_map(
        shards,
        mesh=split,
        in_specs=(
            P(ctx, None),
            P(None, "head"),
            P(None, "head"),
            P(ctx, "head"),
            P(ctx, "head"),
            P(ctx),
            P(),
        ),
        out_specs=(P(ctx, "head"), P(ctx, "head")),
        check_vma=False,
    )
```

```python
import functools
import math

import jax
import jax.numpy as jnp
from jax import lax
from jax.experimental import pallas as pl
from jax.experimental.pallas import tpu as pltpu
from jax.sharding import Mesh
from jax.sharding import PartitionSpec as P

rope_base = 500000.0
big_negative = -1e30
n_ctx = 64
n_head = 4
block_len = 64
key_span = 256
granule = 16
item_group = 3
log2e = 1.4426950408889634


swap = [(0, 1), (1, 0)]
both_swap = [(0, 3), (1, 2), (2, 1), (3, 0)]


def head_perm(s):
    return [(h, (h + s) % n_head) for h in range(n_head)]


def rotation_tables(positions, width):
    half_width = width // 2
    exponent = jnp.arange(half_width, dtype=jnp.float32) * (2.0 / width)
    frequency = jnp.exp(-math.log(rope_base) * exponent)
    angles = positions.astype(jnp.float32)[:, None] * frequency[None, :]
    return (jnp.cos(angles), jnp.sin(angles))


def rotate(vectors, cos_table, sin_table):
    half_width = vectors.shape[1] // 2
    a = vectors[:, :half_width]
    b = vectors[:, half_width:]
    return jnp.concatenate([a * cos_table - b * sin_table, b * cos_table + a * sin_table], axis=1)


def stored_block(place_ref, x, y, rel, block):
    z_at = place_ref[2] ^ (rel // 2)
    core_at = place_ref[3] ^ (rel % 2)
    return ((x * 2 + z_at) * 4 + y) * 4 + core_at * 2 + block


def each_granule(place_ref, order_ref, visit):
    def one_node(node, carry):
        for rel in range(4):
            for block in range(2):
                stored = stored_block(place_ref, node // 4, node % 4, rel, block)
                visit(order_ref[stored], node * 8 + rel * 2 + block)
        return carry

    lax.fori_loop(0, 16, one_node, 0, unroll=2)


def granule_rows(index):
    return pl.ds(pl.multiple_of(index * granule, granule), granule)


def load_operands(place_ref, order_ref, gathered, packs, kv, q_rows, g_rows, starts):
    tokens = kv.shape[0] - key_span
    kv[tokens:, :] = jnp.zeros_like(kv[tokens:, :])

    def fetch(seq, entry):
        kv[granule_rows(seq), :] = gathered[granule_rows(entry), :]

    each_granule(place_ref, order_ref, fetch)
    head_dim = q_rows.shape[1]
    half = starts.shape[1]
    for rel in range(4):
        pack = packs[rel]
        code = pack[256:272, :].astype(jnp.float32)
        start = (code[0:1, :] * 128.0 + code[1:2, :]).astype(jnp.int32)
        for block in range(2):
            part = rel * 2 + block
            starts[part : part + 1, :] = start[:, block * half : (block + 1) * half]
            for group in range(half // block_len):
                to = pl.ds(part * half + group * block_len, block_len)
                cols = pl.ds(group * head_dim, head_dim)
                q_rows[to, :] = pack[block * block_len : (block + 1) * block_len, cols]
                g_rows[to, :] = pack[128 + block * block_len : 128 + (block + 1) * block_len, cols]


contract_last = (((1,), (1,)), ((), ()))


def part_block(place_ref, order_ref, part):
    return order_ref[stored_block(place_ref, place_ref[0], place_ref[1], part // 2, part % 2)]


def part_slot(place_ref, part):
    return ((place_ref[2] * 2 + place_ref[3]) ^ (part // 2)) * 2 + part % 2


def list_items(place_ref, order_ref, starts, items):
    filled = 0
    for part in range(8):
        block = part_block(place_ref, order_ref, part)
        first = jnp.min(starts[part : part + 1, :]) // block_len
        count = (block - first + key_span // granule) // (key_span // granule)

        def add(k, at, part=part, block=block, first=first):
            items[0, at] = part
            items[1, at] = first + k * (key_span // granule)
            items[2, at] = block * block_len
            return at + 1

        filled = lax.fori_loop(0, count, add, filled)
    for spare in range(item_group - 1):
        items[0, filled + spare] = 7
        items[1, filled + spare] = 16 * 8
        items[2, filled + spare] = 0
    return (filled + item_group - 1) // item_group


def fill_positions(key_rel):
    row = lax.broadcasted_iota(jnp.int32, key_rel.shape, 0)
    key_rel[...] = (row // granule) * block_len + row % granule


def item_terms(i, items, place_ref, kv, q_rows, g_rows, starts, key_rel, factor):
    part, first = items[0, i], items[1, i]
    half = starts.shape[1]
    head_dim = q_rows.shape[1]
    rows = pl.ds(pl.multiple_of(first * granule, granule), key_span)
    cols = pl.ds(pl.multiple_of(part * half, half), half)
    offset = first * block_len + (place_ref[2] * 2 + place_ref[3]) * granule
    key = kv[rows, : 2 * head_dim]
    value = kv[rows, 2 * head_dim :]
    q_part = q_rows[cols, :]
    g_part = g_rows[cols, :]
    score = lax.dot_general(
        key,
        jnp.concatenate([q_part, q_part], axis=1),
        contract_last,
        preferred_element_type=jnp.float32,
    )
    prob_grad = lax.dot_general(value, g_part, contract_last, preferred_element_type=jnp.float32)
    lane = lax.broadcasted_iota(jnp.int32, (1, half), 1) % block_len
    end = lane + (items[2, i] - offset)
    start = starts[pl.ds(part, 1), :] - offset
    live = (key_rel[...] <= end) & (key_rel[...] >= start)
    return part, rows, key, q_part, g_part, score * factor, prob_grad, live


def stats_kernel(place_ref, order_ref, *refs, factor):
    gathered, packs, stats_ref = refs[0], refs[1:5], refs[5]
    kv, q_rows, g_rows, starts, key_rel, items, tops, totals, weights = refs[6:]
    load_operands(place_ref, order_ref, gathered, packs, kv, q_rows, g_rows, starts)
    fill_positions(key_rel)
    tops[...] = jnp.full_like(tops, big_negative)
    totals[...] = jnp.zeros_like(totals)
    weights[...] = jnp.zeros_like(weights)
    step_count = list_items(place_ref, order_ref, starts, items)

    def one_step(step, carry):
        both = [
            item_terms(
                item_group * step + i, items, place_ref, kv, q_rows, g_rows, starts, key_rel, factor
            )
            for i in range(item_group)
        ]
        for part, _, _, _, _, score, prob_grad, live in both:
            at = pl.ds(part, 1)
            top = tops[at, :]
            score = jnp.where(live, score, big_negative)
            new_top = jnp.maximum(top, jnp.max(score, axis=0, keepdims=True))
            growth = jnp.exp2(score - new_top)
            faded = jnp.exp2(top - new_top)
            tops[at, :] = new_top
            totals[at, :] = totals[at, :] * faded + jnp.sum(growth, axis=0, keepdims=True)
            weights[at, :] = weights[at, :] * faded + jnp.sum(
                growth * prob_grad, axis=0, keepdims=True
            )
        return carry

    lax.fori_loop(0, step_count, one_step, 0)
    for part in range(8):
        slot = part_slot(place_ref, part)
        at = slice(part, part + 1)
        stats_ref[pl.ds(slot, 1), :] = tops[at, :] + jnp.log2(totals[at, :])
        stats_ref[pl.ds(8 + slot, 1), :] = weights[at, :] / totals[at, :]


def grads_kernel(place_ref, order_ref, *refs, factor, scaling):
    gathered, packs, stats = refs[0], refs[1:5], refs[5:9]
    out_ref, dq_own, dq_others = refs[9], refs[10], refs[11:14]
    kv, q_rows, g_rows, starts, key_rel, items, acc, dq_acc, logs, deltas = refs[14:24]
    out_buf, own_buf, *other_bufs, sems = refs[24:]
    dq_bufs = (own_buf, *other_bufs)
    copies = [
        pltpu.make_async_copy(buf, ref, sems.at[i])
        for i, (buf, ref) in enumerate(zip((*dq_bufs, out_buf), (dq_own, *dq_others, out_ref)))
    ]
    load_operands(place_ref, order_ref, gathered, packs, kv, q_rows, g_rows, starts)
    half = starts.shape[1]
    head_dim = q_rows.shape[1]
    acc[...] = jnp.zeros_like(acc)
    fill_positions(key_rel)

    top = jnp.maximum(
        jnp.maximum(stats[0][:8, :], stats[1][:8, :]), jnp.maximum(stats[2][:8, :], stats[3][:8, :])
    )
    total = jnp.zeros_like(top)
    weighted = jnp.zeros_like(top)
    for s in stats:
        share = jnp.exp2(s[:8, :] - top)
        total = total + share
        weighted = weighted + share * s[8:, :]
    logs[...] = top + jnp.log2(total)
    deltas[...] = weighted / total

    dq_acc[...] = jnp.zeros_like(dq_acc)
    step_count = list_items(place_ref, order_ref, starts, items)
    quarter = place_ref[2] * 2 + place_ref[3]

    def one_step(step, carry):
        both = [
            item_terms(
                item_group * step + i, items, place_ref, kv, q_rows, g_rows, starts, key_rel, factor
            )
            for i in range(item_group)
        ]
        results = []
        for part, rows, key, q_part, g_part, score, prob_grad, live in both:
            slot = pl.ds((quarter ^ (part // 2)) * 2 + part % 2, 1)
            prob = jnp.where(live, jnp.exp2(score - logs[slot, :]), 0.0)
            score_grad = (prob * ((prob_grad - deltas[slot, :]) * scaling)).astype(jnp.bfloat16)
            key_part = jnp.dot(score_grad, q_part, preferred_element_type=jnp.float32)
            value_part = jnp.dot(
                prob.astype(jnp.bfloat16), g_part, preferred_element_type=jnp.float32
            )
            query_part = jnp.dot(key.T, score_grad, preferred_element_type=jnp.float32)
            results.append((part, rows, key_part, value_part, query_part))
        for part, rows, key_part, value_part, query_part in results:
            acc[rows, :head_dim] += key_part
            acc[rows, head_dim:] += value_part
            at = pl.ds(pl.multiple_of(part * head_dim, head_dim), head_dim)
            dq_acc[at, :] += query_part[:head_dim, :] + query_part[head_dim:, :]
        return carry

    lax.fori_loop(0, step_count, one_step, 0)
    for part in range(8):
        dq = dq_acc[part * head_dim : (part + 1) * head_dim, :].T
        rel, block = part // 2, part % 2
        buf = dq_bufs[rel]
        for group in range(half // block_len):
            buf[block * block_len : (block + 1) * block_len, pl.ds(group * head_dim, head_dim)] = (
                dq[group * block_len : (group + 1) * block_len, :].astype(buf.dtype)
            )
        if block == 1:
            copies[rel].start()

    def store(seq, entry):
        out_buf[granule_rows(entry), :] = acc[granule_rows(seq), :].astype(jnp.bfloat16)

    each_granule(place_ref, order_ref, store)
    copies[4].start()
    for copy in copies:
        copy.wait()


def kernel_scratch(quarter, head_dim, rows):
    half = rows // 2
    return [
        pltpu.VMEM((quarter + key_span, 3 * head_dim), jnp.bfloat16),
        pltpu.VMEM((4 * rows, head_dim), jnp.bfloat16),
        pltpu.VMEM((4 * rows, head_dim), jnp.bfloat16),
        pltpu.VMEM((8, half), jnp.int32),
        pltpu.VMEM((key_span, half), jnp.int32),
        pltpu.SMEM((3, 64), jnp.int32),
    ]


def run_stats(place, order, gathered, packs, scaling, tokens, head_dim, rows):
    smem = pl.BlockSpec(memory_space=pltpu.SMEM)
    vmem = pl.BlockSpec(memory_space=pltpu.VMEM)
    return pl.pallas_call(
        functools.partial(stats_kernel, factor=scaling * log2e),
        out_shape=jax.ShapeDtypeStruct((16, rows // 2), jnp.float32),
        in_specs=[smem, smem] + [vmem] * 5,
        out_specs=vmem,
        scratch_shapes=kernel_scratch(tokens // 4, head_dim, rows)
        + [pltpu.VMEM((8, rows // 2), jnp.float32)] * 3,
        compiler_params=pltpu.CompilerParams(vmem_limit_bytes=32 * 1024 * 1024),
        cost_estimate=pl.CostEstimate(
            flops=8 * rows * tokens * head_dim,
            bytes_accessed=4 * 1024 * 1024,
            transcendentals=rows * tokens // 2,
        ),
    )(place, order, gathered, *packs)


def run_grads(place, order, gathered, packs, stats, scaling, tokens, head_dim, rows):
    smem = pl.BlockSpec(memory_space=pltpu.SMEM)
    vmem = pl.BlockSpec(memory_space=pltpu.VMEM)
    quarter = tokens // 4
    half = rows // 2
    return pl.pallas_call(
        functools.partial(grads_kernel, factor=scaling * log2e, scaling=scaling),
        out_shape=[
            jax.ShapeDtypeStruct((quarter, 2 * head_dim), jnp.bfloat16),
            jax.ShapeDtypeStruct((2 * block_len, (half // block_len) * head_dim), jnp.float32),
        ]
        + [jax.ShapeDtypeStruct((2 * block_len, (half // block_len) * head_dim), jnp.bfloat16)] * 3,
        in_specs=[smem, smem] + [vmem] * 9,
        out_specs=[pl.BlockSpec(memory_space=pltpu.HBM)] * 5,
        scratch_shapes=kernel_scratch(quarter, head_dim, rows)
        + [
            pltpu.VMEM((quarter + key_span, 2 * head_dim), jnp.float32),
            pltpu.VMEM((8 * head_dim, half), jnp.float32),
            pltpu.VMEM((8, half), jnp.float32),
            pltpu.VMEM((8, half), jnp.float32),
            pltpu.VMEM((quarter, 2 * head_dim), jnp.bfloat16),
            pltpu.VMEM((2 * block_len, (half // block_len) * head_dim), jnp.float32),
        ]
        + [pltpu.VMEM((2 * block_len, (half // block_len) * head_dim), jnp.bfloat16)] * 3
        + [pltpu.SemaphoreType.DMA((5,))],
        compiler_params=pltpu.CompilerParams(vmem_limit_bytes=57 * 1024 * 1024),
        cost_estimate=pl.CostEstimate(
            flops=4 * rows * tokens * head_dim,
            bytes_accessed=8 * 1024 * 1024,
            transcendentals=rows * tokens // 2,
        ),
    )(place, order, gathered, *packs, *stats)


def finish_kernel(place_ref, parts_ref, cos_ref, sin_ref, out_ref):
    head_dim = cos_ref.shape[1]
    rows = out_ref.shape[1]
    for rel in range(4):
        at = pl.ds(rel * rows, rows)
        total = parts_ref[0, at, :].astype(jnp.float32)
        for i in range(1, parts_ref.shape[0]):
            total += parts_ref[i, at, :].astype(jnp.float32)
        key = total[:, :head_dim]
        key = key * cos_ref[at, :] + pltpu.roll(key, head_dim // 2, 1) * sin_ref[at, :]
        back = jnp.concatenate([key, total[:, head_dim:]], axis=1).astype(jnp.bfloat16)
        owner = (place_ref[0] ^ rel) * n_head
        for head in range(n_head):
            out_ref[owner + head] = back


def run_finish(place, parts, cos_wide, sin_wide):
    smem = pl.BlockSpec(memory_space=pltpu.SMEM)
    vmem = pl.BlockSpec(memory_space=pltpu.VMEM)
    _, rows, width = parts.shape
    return pl.pallas_call(
        finish_kernel,
        out_shape=jax.ShapeDtypeStruct((4 * n_head, rows // 4, width), jnp.bfloat16),
        in_specs=[smem] + [vmem] * 3,
        out_specs=vmem,
        compiler_params=pltpu.CompilerParams(vmem_limit_bytes=16 * 1024 * 1024),
        cost_estimate=pl.CostEstimate(
            flops=20 * rows * width, bytes_accessed=2 * 1024 * 1024, transcendentals=0
        ),
    )(place, parts, cos_wide, sin_wide)


def product_kernel(place_ref, back_ref, own_ref, mine_ref, other_ref, out_ref, *left):
    left_own, left_mine, left_other = left
    width = back_ref.shape[2]
    head_dim = width // 2
    first = pl.multiple_of(place_ref[1] * head_dim, head_dim)
    second = pl.multiple_of(head_dim - first, head_dim)
    for shift in range(n_head):
        for quarter in range(4):
            sender = quarter * n_head + (place_ref[2] + n_head - shift) % n_head
            for block in range(2):
                to = pl.ds(block * block_len + quarter * granule, granule)
                at = pl.ds(block * granule, granule)
                if shift == 0:
                    left_own[to, :] = back_ref[sender, at, :]
                else:
                    cols = pl.ds((shift - 1) * head_dim, head_dim)
                    left_mine[to, cols] = back_ref[sender, at, pl.ds(first, head_dim)]
                    left_other[to, cols] = back_ref[sender, at, pl.ds(second, head_dim)]

    def times(left, right):
        return lax.dot_general(left[...], right, contract_last, preferred_element_type=jnp.float32)

    for tile in range(out_ref.shape[1] // 512):
        at = pl.ds(tile * 512, 512)
        total = times(left_own, own_ref[at, :])
        total += times(left_mine, mine_ref[at, :])
        total += times(left_other, other_ref[at, :])
        out_ref[:, at] = total.astype(jnp.bfloat16)


def run_product(place, back, own, mine, other):
    smem = pl.BlockSpec(memory_space=pltpu.SMEM)
    vmem = pl.BlockSpec(memory_space=pltpu.VMEM)
    row_count = back.shape[0] * back.shape[1] // n_head
    out_width, depth = mine.shape
    return pl.pallas_call(
        product_kernel,
        out_shape=jax.ShapeDtypeStruct((row_count, out_width), jnp.bfloat16),
        in_specs=[smem] + [vmem] * 4,
        out_specs=vmem,
        scratch_shapes=[pltpu.VMEM((row_count, back.shape[2]), jnp.bfloat16)]
        + [pltpu.VMEM((row_count, depth), jnp.bfloat16)] * 2,
        compiler_params=pltpu.CompilerParams(vmem_limit_bytes=24 * 1024 * 1024),
        cost_estimate=pl.CostEstimate(
            flops=4 * row_count * depth * out_width,
            bytes_accessed=5 * 1024 * 1024,
            transcendentals=0,
        ),
    )(place, back, own, mine, other)


def shards(layer_input, key_weight, value_weight, queries, out_grad, doc_start, block_order):
    f32, bf16 = jnp.float32, jnp.bfloat16
    row_count = layer_input.shape[0]
    tokens = row_count * n_ctx
    head_dim = key_weight.shape[1]
    width = key_weight.shape[0]
    groups = queries.shape[1] // head_dim
    rows = row_count * groups
    scaling = 1.0 / math.sqrt(head_dim)
    x, y = lax.axis_index("x"), lax.axis_index("y")
    z, core, head = lax.axis_index("zl"), lax.axis_index("core"), lax.axis_index("head")
    core_is_one = core == 1

    def pick(v, index, axis):
        return lax.dynamic_index_in_dim(v, index, axis, keepdims=False)

    def blocks_of(z_at, core_at):
        at = ((x * 2 + z_at) * 4 + y) * 4 + core_at * 2
        return lax.dynamic_slice_in_dim(block_order, at, 2)

    own_blocks = blocks_of(z, core)
    own_pos = (
        own_blocks[:, None] * block_len + jnp.arange(block_len, dtype=jnp.int32)[None, :]
    ).reshape(-1)
    cos_own, sin_own = rotation_tables(own_pos, head_dim)
    key_raw = jnp.dot(layer_input, key_weight, preferred_element_type=f32)
    keys = rotate(key_raw, cos_own, sin_own)
    key_hi = lax.reduce_precision(keys, 8, 7)
    key_lo = keys - key_hi
    values = jnp.dot(layer_input, value_weight, preferred_element_type=f32)
    local = jnp.concatenate(
        [key_hi.astype(bf16), key_lo.astype(bf16), values.astype(bf16)], axis=1
    ).reshape(2, 2, 2, granule, 3 * head_dim)

    pair = jnp.stack(
        [pick(local, core, 2), lax.ppermute(pick(local, 1 - core, 2), "core", swap)]
    )

    node = jnp.stack([pick(pair, z, 2), lax.ppermute(pick(pair, 1 - z, 2), "zl", swap)])
    node = node.reshape(1, row_count, 3 * head_dim)

    out_width = width // n_head
    share = out_width // 16
    node_index = x * 4 + y

    def weight_share(w):
        return pick(w.reshape(n_head, 16, share, head_dim), node_index, 1)

    weight_shares = jnp.where(
        core_is_one, weight_share(value_weight), weight_share(key_weight)
    )
    node, weight_shares = lax.optimization_barrier((node, weight_shares))
    weight_rows = [
        lax.ppermute(pick(weight_shares, (head + s) % n_head, 0), "head", head_perm(s))
        for s in (1, 2, 3)
    ]
    weight_rows = jnp.concatenate(weight_rows, axis=1)[None]
    weight_rows = jnp.broadcast_to(weight_rows, (16, share, (n_head - 1) * head_dim))

    def per_column(v):
        return jnp.broadcast_to(v.reshape(2, 1, block_len), (2, groups, block_len)).reshape(1, rows)

    start_cols = per_column(doc_start)
    start_code = jnp.concatenate(
        [start_cols // 128, start_cols % 128, jnp.zeros((14, rows), jnp.int32)], axis=0
    ).astype(bf16)
    pack_own = jnp.concatenate([queries, out_grad, start_code], axis=0)
    pack_z = lax.ppermute(pack_own, "zl", swap)
    pack_z, weight_rows = lax.optimization_barrier((pack_z, weight_rows))
    packs = [
        pack_own,
        lax.ppermute(pack_own, "core", swap),
        pack_z,
        lax.ppermute(pack_z, "core", swap),
    ]

    gathered = lax.all_to_all(
        jnp.broadcast_to(node, (16, row_count, 3 * head_dim)), ("x", "y"), 0, 0
    ).reshape(tokens // 4, 3 * head_dim)
    weights_mine = lax.all_to_all(weight_rows, ("x", "y"), 0, 0)

    quarter = z * 2 + core
    place = jnp.stack([x, y, z, core]).astype(jnp.int32)
    stats = run_stats(place, block_order, gathered, packs, scaling, tokens, head_dim, rows)
    stats_all = [
        stats,
        lax.ppermute(stats, "core", swap),
        lax.ppermute(stats, "zl", swap),
        lax.ppermute(stats, ("zl", "core"), both_swap),
    ]
    grads, dq_own, *dq_others = run_grads(
        place, block_order, gathered, packs, stats_all, scaling, tokens, head_dim, rows
    )
    grads, weights_mine = lax.optimization_barrier((grads, weights_mine))
    weights_mine = weights_mine.reshape(out_width, (n_head - 1) * head_dim)
    weights_other = lax.ppermute(weights_mine, "core", swap)

    weights_own = jnp.concatenate(
        [lax.dynamic_slice_in_dim(w, head * out_width, out_width) for w in (key_weight, value_weight)],
        axis=1,
    )
    grads = lax.all_to_all(
        grads.reshape(16, row_count, 2 * head_dim), ("x", "y"), 0, 0
    )
    node_blocks = jnp.concatenate(
        [blocks_of(z ^ (rel // 2), core ^ (rel % 2)) for rel in range(4)]
    )
    quarter_pos = (
        node_blocks[:, None] * block_len
        + quarter * granule
        + jnp.arange(granule, dtype=jnp.int32)[None, :]
    ).reshape(-1)
    cos_node, sin_node = rotation_tables(quarter_pos, head_dim)

    here = jnp.stack([quarter, core, head]).astype(jnp.int32)
    back = run_finish(
        here,
        grads,
        jnp.concatenate([cos_node, cos_node], axis=1),
        jnp.concatenate([sin_node, -sin_node], axis=1),
    )
    back = lax.all_to_all(back, ("zl", "core", "head"), 0, 0)
    input_grad = run_product(here, back, weights_own, weights_mine, weights_other)

    dq_sum = (
        dq_own
        + lax.ppermute(dq_others[0], "core", swap).astype(f32)
        + lax.ppermute(dq_others[1], "zl", swap).astype(f32)
        + lax.ppermute(dq_others[2], ("zl", "core"), both_swap).astype(f32)
    )
    return (input_grad, dq_sum.astype(bf16))


def solution(mesh):
    ctx = ("x", "zl", "y", "core")
    split = Mesh(mesh.devices.reshape(4, 2, 4, 2, n_head), ctx + ("head",))
    return jax.shard_map(
        shards,
        mesh=split,
        in_specs=(
            P(ctx, None),
            P(None, "head"),
            P(None, "head"),
            P(ctx, "head"),
            P(ctx, "head"),
            P(ctx),
            P(),
        ),
        out_specs=(P(ctx, "head"), P(ctx, "head")),
        check_vma=False,
    )
```

```python
import functools
import math

import jax
import jax.numpy as jnp
from jax import lax
from jax.experimental import pallas as pl
from jax.experimental.pallas import tpu as pltpu
from jax.sharding import Mesh
from jax.sharding import PartitionSpec as P

rope_base = 500000.0
big_negative = -1e30
n_ctx = 64
n_head = 4
block_len = 64
key_span = 192
granule = 16
item_group = 4
log2e = 1.4426950408889634


swap = [(0, 1), (1, 0)]
both_swap = [(0, 3), (1, 2), (2, 1), (3, 0)]


def head_perm(s):
    return [(h, (h + s) % n_head) for h in range(n_head)]


def rotation_tables(positions, width):
    half_width = width // 2
    exponent = jnp.arange(half_width, dtype=jnp.float32) * (2.0 / width)
    frequency = jnp.exp(-math.log(rope_base) * exponent)
    angles = positions.astype(jnp.float32)[:, None] * frequency[None, :]
    return (jnp.cos(angles), jnp.sin(angles))


def rotate(vectors, cos_table, sin_table):
    half_width = vectors.shape[1] // 2
    a = vectors[:, :half_width]
    b = vectors[:, half_width:]
    return jnp.concatenate([a * cos_table - b * sin_table, b * cos_table + a * sin_table], axis=1)


def stored_block(place_ref, x, y, rel, block):
    z_at = place_ref[2] ^ (rel // 2)
    core_at = place_ref[3] ^ (rel % 2)
    return ((x * 2 + z_at) * 4 + y) * 4 + core_at * 2 + block


def each_granule(place_ref, order_ref, visit):
    def one_node(node, carry):
        for rel in range(4):
            for block in range(2):
                stored = stored_block(place_ref, node // 4, node % 4, rel, block)
                visit(order_ref[stored], node * 8 + rel * 2 + block)
        return carry

    lax.fori_loop(0, 16, one_node, 0, unroll=2)


def granule_rows(index):
    return pl.ds(pl.multiple_of(index * granule, granule), granule)


def load_operands(place_ref, order_ref, gathered, packs, kv, q_rows, g_rows, starts):
    tokens = kv.shape[0] - key_span
    kv[tokens:, :] = jnp.zeros_like(kv[tokens:, :])

    def fetch(seq, entry):
        kv[granule_rows(seq), :] = gathered[granule_rows(entry), :]

    each_granule(place_ref, order_ref, fetch)
    head_dim = q_rows.shape[1]
    half = starts.shape[1]
    for rel in range(4):
        pack = packs[rel]
        code = pack[256:272, :].astype(jnp.float32)
        start = (code[0:1, :] * 128.0 + code[1:2, :]).astype(jnp.int32)
        for block in range(2):
            part = rel * 2 + block
            starts[part : part + 1, :] = start[:, block * half : (block + 1) * half]
            for group in range(half // block_len):
                to = pl.ds(part * half + group * block_len, block_len)
                cols = pl.ds(group * head_dim, head_dim)
                q_rows[to, :] = pack[block * block_len : (block + 1) * block_len, cols]
                g_rows[to, :] = pack[128 + block * block_len : 128 + (block + 1) * block_len, cols]


contract_last = (((1,), (1,)), ((), ()))


def part_block(place_ref, order_ref, part):
    return order_ref[stored_block(place_ref, place_ref[0], place_ref[1], part // 2, part % 2)]


def part_slot(place_ref, part):
    return ((place_ref[2] * 2 + place_ref[3]) ^ (part // 2)) * 2 + part % 2


def list_items(place_ref, order_ref, starts, items):
    filled = 0
    for part in range(8):
        block = part_block(place_ref, order_ref, part)
        first = jnp.min(starts[part : part + 1, :]) // block_len
        count = (block - first + key_span // granule) // (key_span // granule)

        def add(k, at, part=part, block=block, first=first):
            items[0, at] = part
            items[1, at] = first + k * (key_span // granule)
            items[2, at] = block * block_len
            return at + 1

        filled = lax.fori_loop(0, count, add, filled)
    for spare in range(item_group - 1):
        items[0, filled + spare] = 7
        items[1, filled + spare] = 16 * 8
        items[2, filled + spare] = 0
    return (filled + item_group - 1) // item_group


def fill_positions(key_rel):
    row = lax.broadcasted_iota(jnp.int32, key_rel.shape, 0)
    key_rel[...] = (row // granule) * block_len + row % granule


def item_terms(i, items, place_ref, kv, q_rows, g_rows, starts, key_rel, factor):
    part, first = items[0, i], items[1, i]
    half = starts.shape[1]
    head_dim = q_rows.shape[1]
    rows = pl.ds(pl.multiple_of(first * granule, granule), key_span)
    cols = pl.ds(pl.multiple_of(part * half, half), half)
    offset = first * block_len + (place_ref[2] * 2 + place_ref[3]) * granule
    key = kv[rows, : 2 * head_dim]
    value = kv[rows, 2 * head_dim :]
    q_part = q_rows[cols, :]
    g_part = g_rows[cols, :]
    score = lax.dot_general(
        key,
        jnp.concatenate([q_part, q_part], axis=1),
        contract_last,
        preferred_element_type=jnp.float32,
    )
    prob_grad = lax.dot_general(value, g_part, contract_last, preferred_element_type=jnp.float32)
    lane = lax.broadcasted_iota(jnp.int32, (1, half), 1) % block_len
    end = lane + (items[2, i] - offset)
    start = starts[pl.ds(part, 1), :] - offset
    live = (key_rel[...] <= end) & (key_rel[...] >= start)
    return part, rows, key, q_part, g_part, score * factor, prob_grad, live


def stats_kernel(place_ref, order_ref, *refs, factor):
    gathered, packs, stats_ref = refs[0], refs[1:5], refs[5]
    kv, q_rows, g_rows, starts, key_rel, items, tops, totals, weights = refs[6:]
    load_operands(place_ref, order_ref, gathered, packs, kv, q_rows, g_rows, starts)
    fill_positions(key_rel)
    tops[...] = jnp.full_like(tops, big_negative)
    totals[...] = jnp.zeros_like(totals)
    weights[...] = jnp.zeros_like(weights)
    step_count = list_items(place_ref, order_ref, starts, items)

    def one_step(step, carry):
        both = [
            item_terms(
                item_group * step + i, items, place_ref, kv, q_rows, g_rows, starts, key_rel, factor
            )
            for i in range(item_group)
        ]
        for part, _, _, _, _, score, prob_grad, live in both:
            at = pl.ds(part, 1)
            top = tops[at, :]
            score = jnp.where(live, score, big_negative)
            new_top = jnp.maximum(top, jnp.max(score, axis=0, keepdims=True))
            growth = jnp.exp2(score - new_top)
            faded = jnp.exp2(top - new_top)
            tops[at, :] = new_top
            totals[at, :] = totals[at, :] * faded + jnp.sum(growth, axis=0, keepdims=True)
            weights[at, :] = weights[at, :] * faded + jnp.sum(
                growth * prob_grad, axis=0, keepdims=True
            )
        return carry

    lax.fori_loop(0, step_count, one_step, 0)
    for part in range(8):
        slot = part_slot(place_ref, part)
        at = slice(part, part + 1)
        stats_ref[pl.ds(slot, 1), :] = tops[at, :] + jnp.log2(totals[at, :])
        stats_ref[pl.ds(8 + slot, 1), :] = weights[at, :] / totals[at, :]


def grads_kernel(place_ref, order_ref, *refs, factor, scaling):
    gathered, packs, stats = refs[0], refs[1:5], refs[5:9]
    out_ref, dq_own, dq_others = refs[9], refs[10], refs[11:14]
    kv, q_rows, g_rows, starts, key_rel, items, acc, dq_acc, logs, deltas = refs[14:24]
    out_buf, own_buf, *other_bufs, sems = refs[24:]
    dq_bufs = (own_buf, *other_bufs)
    copies = [
        pltpu.make_async_copy(buf, ref, sems.at[i])
        for i, (buf, ref) in enumerate(zip((*dq_bufs, out_buf), (dq_own, *dq_others, out_ref)))
    ]
    load_operands(place_ref, order_ref, gathered, packs, kv, q_rows, g_rows, starts)
    half = starts.shape[1]
    head_dim = q_rows.shape[1]
    acc[...] = jnp.zeros_like(acc)
    fill_positions(key_rel)

    top = jnp.maximum(
        jnp.maximum(stats[0][:8, :], stats[1][:8, :]), jnp.maximum(stats[2][:8, :], stats[3][:8, :])
    )
    total = jnp.zeros_like(top)
    weighted = jnp.zeros_like(top)
    for s in stats:
        share = jnp.exp2(s[:8, :] - top)
        total = total + share
        weighted = weighted + share * s[8:, :]
    logs[...] = top + jnp.log2(total)
    deltas[...] = weighted / total

    dq_acc[...] = jnp.zeros_like(dq_acc)
    step_count = list_items(place_ref, order_ref, starts, items)
    quarter = place_ref[2] * 2 + place_ref[3]

    def one_step(step, carry):
        both = [
            item_terms(
                item_group * step + i, items, place_ref, kv, q_rows, g_rows, starts, key_rel, factor
            )
            for i in range(item_group)
        ]
        results = []
        for part, rows, key, q_part, g_part, score, prob_grad, live in both:
            slot = pl.ds((quarter ^ (part // 2)) * 2 + part % 2, 1)
            prob = jnp.where(live, jnp.exp2(score - logs[slot, :]), 0.0)
            score_grad = (prob * ((prob_grad - deltas[slot, :]) * scaling)).astype(jnp.bfloat16)
            key_part = jnp.dot(score_grad, q_part, preferred_element_type=jnp.float32)
            value_part = jnp.dot(
                prob.astype(jnp.bfloat16), g_part, preferred_element_type=jnp.float32
            )
            query_part = jnp.dot(key.T, score_grad, preferred_element_type=jnp.float32)
            results.append((part, rows, key_part, value_part, query_part))
        for part, rows, key_part, value_part, query_part in results:
            acc[rows, :head_dim] += key_part
            acc[rows, head_dim:] += value_part
            at = pl.ds(pl.multiple_of(part * head_dim, head_dim), head_dim)
            dq_acc[at, :] += query_part[:head_dim, :] + query_part[head_dim:, :]
        return carry

    lax.fori_loop(0, step_count, one_step, 0)
    for part in range(8):
        dq = dq_acc[part * head_dim : (part + 1) * head_dim, :].T
        rel, block = part // 2, part % 2
        buf = dq_bufs[rel]
        for group in range(half // block_len):
            buf[block * block_len : (block + 1) * block_len, pl.ds(group * head_dim, head_dim)] = (
                dq[group * block_len : (group + 1) * block_len, :].astype(buf.dtype)
            )
        if block == 1:
            copies[rel].start()

    def store(seq, entry):
        out_buf[granule_rows(entry), :] = acc[granule_rows(seq), :].astype(jnp.bfloat16)

    each_granule(place_ref, order_ref, store)
    copies[4].start()
    for copy in copies:
        copy.wait()


def kernel_scratch(quarter, head_dim, rows):
    half = rows // 2
    return [
        pltpu.VMEM((quarter + key_span, 3 * head_dim), jnp.bfloat16),
        pltpu.VMEM((4 * rows, head_dim), jnp.bfloat16),
        pltpu.VMEM((4 * rows, head_dim), jnp.bfloat16),
        pltpu.VMEM((8, half), jnp.int32),
        pltpu.VMEM((key_span, half), jnp.int32),
        pltpu.SMEM((3, 128), jnp.int32),
    ]


def run_stats(place, order, gathered, packs, scaling, tokens, head_dim, rows):
    smem = pl.BlockSpec(memory_space=pltpu.SMEM)
    vmem = pl.BlockSpec(memory_space=pltpu.VMEM)
    return pl.pallas_call(
        functools.partial(stats_kernel, factor=scaling * log2e),
        out_shape=jax.ShapeDtypeStruct((16, rows // 2), jnp.float32),
        in_specs=[smem, smem] + [vmem] * 5,
        out_specs=vmem,
        scratch_shapes=kernel_scratch(tokens // 4, head_dim, rows)
        + [pltpu.VMEM((8, rows // 2), jnp.float32)] * 3,
        compiler_params=pltpu.CompilerParams(vmem_limit_bytes=32 * 1024 * 1024),
        cost_estimate=pl.CostEstimate(
            flops=8 * rows * tokens * head_dim,
            bytes_accessed=4 * 1024 * 1024,
            transcendentals=rows * tokens // 2,
        ),
    )(place, order, gathered, *packs)


def run_grads(place, order, gathered, packs, stats, scaling, tokens, head_dim, rows):
    smem = pl.BlockSpec(memory_space=pltpu.SMEM)
    vmem = pl.BlockSpec(memory_space=pltpu.VMEM)
    quarter = tokens // 4
    half = rows // 2
    return pl.pallas_call(
        functools.partial(grads_kernel, factor=scaling * log2e, scaling=scaling),
        out_shape=[
            jax.ShapeDtypeStruct((quarter, 2 * head_dim), jnp.bfloat16),
            jax.ShapeDtypeStruct((2 * block_len, (half // block_len) * head_dim), jnp.float32),
        ]
        + [jax.ShapeDtypeStruct((2 * block_len, (half // block_len) * head_dim), jnp.bfloat16)] * 3,
        in_specs=[smem, smem] + [vmem] * 9,
        out_specs=[pl.BlockSpec(memory_space=pltpu.HBM)] * 5,
        scratch_shapes=kernel_scratch(quarter, head_dim, rows)
        + [
            pltpu.VMEM((quarter + key_span, 2 * head_dim), jnp.float32),
            pltpu.VMEM((8 * head_dim, half), jnp.float32),
            pltpu.VMEM((8, half), jnp.float32),
            pltpu.VMEM((8, half), jnp.float32),
            pltpu.VMEM((quarter, 2 * head_dim), jnp.bfloat16),
            pltpu.VMEM((2 * block_len, (half // block_len) * head_dim), jnp.float32),
        ]
        + [pltpu.VMEM((2 * block_len, (half // block_len) * head_dim), jnp.bfloat16)] * 3
        + [pltpu.SemaphoreType.DMA((5,))],
        compiler_params=pltpu.CompilerParams(vmem_limit_bytes=57 * 1024 * 1024),
        cost_estimate=pl.CostEstimate(
            flops=4 * rows * tokens * head_dim,
            bytes_accessed=8 * 1024 * 1024,
            transcendentals=rows * tokens // 2,
        ),
    )(place, order, gathered, *packs, *stats)


def finish_kernel(place_ref, parts_ref, cos_ref, sin_ref, out_ref):
    head_dim = cos_ref.shape[1]
    rows = out_ref.shape[1]
    for rel in range(4):
        at = pl.ds(rel * rows, rows)
        total = parts_ref[0, at, :].astype(jnp.float32)
        for i in range(1, parts_ref.shape[0]):
            total += parts_ref[i, at, :].astype(jnp.float32)
        key = total[:, :head_dim]
        key = key * cos_ref[at, :] + pltpu.roll(key, head_dim // 2, 1) * sin_ref[at, :]
        back = jnp.concatenate([key, total[:, head_dim:]], axis=1).astype(jnp.bfloat16)
        owner = (place_ref[0] ^ rel) * n_head
        for head in range(n_head):
            out_ref[owner + head] = back


def run_finish(place, parts, cos_wide, sin_wide):
    smem = pl.BlockSpec(memory_space=pltpu.SMEM)
    vmem = pl.BlockSpec(memory_space=pltpu.VMEM)
    _, rows, width = parts.shape
    return pl.pallas_call(
        finish_kernel,
        out_shape=jax.ShapeDtypeStruct((4 * n_head, rows // 4, width), jnp.bfloat16),
        in_specs=[smem] + [vmem] * 3,
        out_specs=vmem,
        compiler_params=pltpu.CompilerParams(vmem_limit_bytes=16 * 1024 * 1024),
        cost_estimate=pl.CostEstimate(
            flops=20 * rows * width, bytes_accessed=2 * 1024 * 1024, transcendentals=0
        ),
    )(place, parts, cos_wide, sin_wide)


def product_kernel(place_ref, back_ref, own_ref, mine_ref, other_ref, out_ref, *left):
    left_own, left_mine, left_other = left
    width = back_ref.shape[2]
    head_dim = width // 2
    first = pl.multiple_of(place_ref[1] * head_dim, head_dim)
    second = pl.multiple_of(head_dim - first, head_dim)
    for shift in range(n_head):
        for quarter in range(4):
            sender = quarter * n_head + (place_ref[2] + n_head - shift) % n_head
            for block in range(2):
                to = pl.ds(block * block_len + quarter * granule, granule)
                at = pl.ds(block * granule, granule)
                if shift == 0:
                    left_own[to, :] = back_ref[sender, at, :]
                else:
                    cols = pl.ds((shift - 1) * head_dim, head_dim)
                    left_mine[to, cols] = back_ref[sender, at, pl.ds(first, head_dim)]
                    left_other[to, cols] = back_ref[sender, at, pl.ds(second, head_dim)]

    def times(left, right):
        return lax.dot_general(left[...], right, contract_last, preferred_element_type=jnp.float32)

    for tile in range(out_ref.shape[1] // 512):
        at = pl.ds(tile * 512, 512)
        total = times(left_own, own_ref[at, :])
        total += times(left_mine, mine_ref[at, :])
        total += times(left_other, other_ref[at, :])
        out_ref[:, at] = total.astype(jnp.bfloat16)


def run_product(place, back, own, mine, other):
    smem = pl.BlockSpec(memory_space=pltpu.SMEM)
    vmem = pl.BlockSpec(memory_space=pltpu.VMEM)
    row_count = back.shape[0] * back.shape[1] // n_head
    out_width, depth = mine.shape
    return pl.pallas_call(
        product_kernel,
        out_shape=jax.ShapeDtypeStruct((row_count, out_width), jnp.bfloat16),
        in_specs=[smem] + [vmem] * 4,
        out_specs=vmem,
        scratch_shapes=[pltpu.VMEM((row_count, back.shape[2]), jnp.bfloat16)]
        + [pltpu.VMEM((row_count, depth), jnp.bfloat16)] * 2,
        compiler_params=pltpu.CompilerParams(vmem_limit_bytes=24 * 1024 * 1024),
        cost_estimate=pl.CostEstimate(
            flops=4 * row_count * depth * out_width,
            bytes_accessed=5 * 1024 * 1024,
            transcendentals=0,
        ),
    )(place, back, own, mine, other)


def shards(layer_input, key_weight, value_weight, queries, out_grad, doc_start, block_order):
    f32, bf16 = jnp.float32, jnp.bfloat16
    row_count = layer_input.shape[0]
    tokens = row_count * n_ctx
    head_dim = key_weight.shape[1]
    width = key_weight.shape[0]
    groups = queries.shape[1] // head_dim
    rows = row_count * groups
    scaling = 1.0 / math.sqrt(head_dim)
    x, y = lax.axis_index("x"), lax.axis_index("y")
    z, core, head = lax.axis_index("zl"), lax.axis_index("core"), lax.axis_index("head")
    core_is_one = core == 1

    def pick(v, index, axis):
        return lax.dynamic_index_in_dim(v, index, axis, keepdims=False)

    def blocks_of(z_at, core_at):
        at = ((x * 2 + z_at) * 4 + y) * 4 + core_at * 2
        return lax.dynamic_slice_in_dim(block_order, at, 2)

    own_blocks = blocks_of(z, core)
    own_pos = (
        own_blocks[:, None] * block_len + jnp.arange(block_len, dtype=jnp.int32)[None, :]
    ).reshape(-1)
    cos_own, sin_own = rotation_tables(own_pos, head_dim)
    key_raw = jnp.dot(layer_input, key_weight, preferred_element_type=f32)
    keys = rotate(key_raw, cos_own, sin_own)
    key_hi = lax.reduce_precision(keys, 8, 7)
    key_lo = keys - key_hi
    values = jnp.dot(layer_input, value_weight, preferred_element_type=f32)
    local = jnp.concatenate(
        [key_hi.astype(bf16), key_lo.astype(bf16), values.astype(bf16)], axis=1
    ).reshape(2, 2, 2, granule, 3 * head_dim)

    pair = jnp.stack(
        [pick(local, core, 2), lax.ppermute(pick(local, 1 - core, 2), "core", swap)]
    )

    node = jnp.stack([pick(pair, z, 2), lax.ppermute(pick(pair, 1 - z, 2), "zl", swap)])
    node = node.reshape(1, row_count, 3 * head_dim)

    out_width = width // n_head
    share = out_width // 16
    node_index = x * 4 + y

    def weight_share(w):
        return pick(w.reshape(n_head, 16, share, head_dim), node_index, 1)

    weight_shares = jnp.where(
        core_is_one, weight_share(value_weight), weight_share(key_weight)
    )
    node, weight_shares = lax.optimization_barrier((node, weight_shares))
    weight_rows = [
        lax.ppermute(pick(weight_shares, (head + s) % n_head, 0), "head", head_perm(s))
        for s in (1, 2, 3)
    ]
    weight_rows = jnp.concatenate(weight_rows, axis=1)[None]
    weight_rows = jnp.broadcast_to(weight_rows, (16, share, (n_head - 1) * head_dim))

    def per_column(v):
        return jnp.broadcast_to(v.reshape(2, 1, block_len), (2, groups, block_len)).reshape(1, rows)

    start_cols = per_column(doc_start)
    start_code = jnp.concatenate(
        [start_cols // 128, start_cols % 128, jnp.zeros((14, rows), jnp.int32)], axis=0
    ).astype(bf16)
    pack_own = jnp.concatenate([queries, out_grad, start_code], axis=0)
    pack_z = lax.ppermute(pack_own, "zl", swap)
    pack_z, weight_rows = lax.optimization_barrier((pack_z, weight_rows))
    packs = [
        pack_own,
        lax.ppermute(pack_own, "core", swap),
        pack_z,
        lax.ppermute(pack_z, "core", swap),
    ]

    gathered = lax.all_to_all(
        jnp.broadcast_to(node, (16, row_count, 3 * head_dim)), ("x", "y"), 0, 0
    ).reshape(tokens // 4, 3 * head_dim)
    weights_mine = lax.all_to_all(weight_rows, ("x", "y"), 0, 0)

    quarter = z * 2 + core
    place = jnp.stack([x, y, z, core]).astype(jnp.int32)
    stats = run_stats(place, block_order, gathered, packs, scaling, tokens, head_dim, rows)
    stats_all = [
        stats,
        lax.ppermute(stats, "core", swap),
        lax.ppermute(stats, "zl", swap),
        lax.ppermute(stats, ("zl", "core"), both_swap),
    ]
    grads, dq_own, *dq_others = run_grads(
        place, block_order, gathered, packs, stats_all, scaling, tokens, head_dim, rows
    )
    grads, weights_mine = lax.optimization_barrier((grads, weights_mine))
    weights_mine = weights_mine.reshape(out_width, (n_head - 1) * head_dim)
    weights_other = lax.ppermute(weights_mine, "core", swap)

    weights_own = jnp.concatenate(
        [lax.dynamic_slice_in_dim(w, head * out_width, out_width) for w in (key_weight, value_weight)],
        axis=1,
    )
    grads = lax.all_to_all(
        grads.reshape(16, row_count, 2 * head_dim), ("x", "y"), 0, 0
    )
    node_blocks = jnp.concatenate(
        [blocks_of(z ^ (rel // 2), core ^ (rel % 2)) for rel in range(4)]
    )
    quarter_pos = (
        node_blocks[:, None] * block_len
        + quarter * granule
        + jnp.arange(granule, dtype=jnp.int32)[None, :]
    ).reshape(-1)
    cos_node, sin_node = rotation_tables(quarter_pos, head_dim)

    here = jnp.stack([quarter, core, head]).astype(jnp.int32)
    back = run_finish(
        here,
        grads,
        jnp.concatenate([cos_node, cos_node], axis=1),
        jnp.concatenate([sin_node, -sin_node], axis=1),
    )
    back = lax.all_to_all(back, ("zl", "core", "head"), 0, 0)
    input_grad = run_product(here, back, weights_own, weights_mine, weights_other)

    dq_sum = (
        dq_own
        + lax.ppermute(dq_others[0], "core", swap).astype(f32)
        + lax.ppermute(dq_others[1], "zl", swap).astype(f32)
        + lax.ppermute(dq_others[2], ("zl", "core"), both_swap).astype(f32)
    )
    return (input_grad, dq_sum.astype(bf16))


def solution(mesh):
    ctx = ("x", "zl", "y", "core")
    split = Mesh(mesh.devices.reshape(4, 2, 4, 2, n_head), ctx + ("head",))
    return jax.shard_map(
        shards,
        mesh=split,
        in_specs=(
            P(ctx, None),
            P(None, "head"),
            P(None, "head"),
            P(ctx, "head"),
            P(ctx, "head"),
            P(ctx),
            P(),
        ),
        out_specs=(P(ctx, "head"), P(ctx, "head")),
        check_vma=False,
    )
```
